256 devices in a mesh: blk: 64 (over x, z, core), crs: 4 (over y).
Axes of the slice: x: 4, y: 4, z: 8, core: 2. Of those that a mesh axis runs over, the one named last changes fastest.
Arguments:
- positions: float32 [3, 1024, 32, 128], P(None, 'blk', 'crs'), may hold values from 0 to 1
- pressure_start: float32 [1024, 32, 128], P('blk', 'crs'), may hold values from 0 to 2
- source: float32 [1024, 32, 128], P('blk', 'crs'), may hold values from 0.2 to 2
- resist: float32 [1024, 32, 128], P('blk', 'crs'), may hold values from 0.02 to 0.2
- neighbour_tiles: int32 [1024, 32, 6], P('blk', 'crs'), may hold values from 0 to 179, as said below
- pair_owner: int32 [524288, 1], P(('blk', 'crs')), may hold values from 0 to 63; in each aligned block of 2048 rows (0 to 2047, 2048 to 4095, ...) at most 64 rows name the same one
- pair_fluid: int32 [524288], P(('blk', 'crs')), may hold values from 0 to 16383
- pair_grain: int32 [524288], P(('blk', 'crs')), may hold values from 0 to 1023
- pair_normal: float32 [3, 524288], P(None, ('blk', 'crs')), may hold values from -6 to 6
- grain_positions: float32 [3, 262144], P(None, ('blk', 'crs')), may hold values from 0 to 1
- grain_velocity: float32 [3, 262144], P(None, ('blk', 'crs')), may hold values from -6 to 6
- grain_mass: float32 [262144], P(('blk', 'crs')), may hold values from 0.5 to 2
- contact_tiles: int32 [2048, 4], P(('blk', 'crs')), may hold values from 0 to 7
Outputs:
- pressure: float32 [1024, 32, 128], P('blk', 'crs')
- grain_new: float32 [3, 262144], P(None, ('blk', 'crs'))
- pair_velocity: float32 [3, 524288], P(None, ('blk', 'crs'))
The draws below stay inside these ranges and needn't reach their ends.
Inputs may be any that keep to these rules, and one draw needn't show every extreme that they name: `neighbour_tiles`: the entries of one tile are distinct; the first is the tile itself and the others are 5 of its eight neighbouring tiles in the extended grid, in some order. `pair_owner`: among the rows of one device, at most 64 name one owner, a bound that some block reaches.
All inputs are finite; a program needn't handle non-finite values.
Results may differ from the reference program's by a relative error of at most 0.0001.
Values sent between devices are 32-bit elements; how exact they have to be, the bound alone decides.
No kernel may reach another device: no remote copies, remote signals or barrier semaphores. Data moves between devices by JAX's collectives and lax.ppermute only.
A program may use at most 128 MiB of HBM per device.

```python
import math
import jax
import jax.numpy as jnp
import numpy as np
from jax import lax

TX = 16
TY = 8
KN = 6
ITERS = 3
G_DEV = 1024
KG = 4
CP = 2048
CAP = 64
FX = 1024
FY = 32
GRAINS = 262144
GTILES = 2048
PAIRS = 524288
N_BLK = 64
N_CRS = 4


def draw_neighbour_tiles(key, part):
    key = jax.random.fold_in(key, 7)
    scores = jax.random.randint(key, (FX, FY, 8), 0, 2 ** 20) * 16 + jnp.arange(8, dtype=jnp.int32)
    order = jnp.argsort(scores, axis=-1)
    others = jnp.array([0, 1, 2, 3, 5, 6, 7, 8], dtype=jnp.int32)[order][:, :, :KN - 1]
    chosen = jnp.concatenate([jnp.full((FX, FY, 1), 4, jnp.int32), others], axis=-1)
    step_x = chosen // 3 - 1
    step_y = chosen % 3 - 1
    tile_x = (jnp.arange(FX, dtype=jnp.int32) % TX)[:, None, None]
    tile_y = (jnp.arange(FY, dtype=jnp.int32) % TY)[None, :, None]
    return ((tile_x + 1 + step_x) * (TY + 2) + tile_y + 1 + step_y).astype(jnp.int32)


def with_ends(drawn, rng, smallest, top_value):
    place = [jax.random.randint(jax.random.fold_in(rng, axis), (), 0, length) for axis, length in enumerate(drawn.shape)]
    widest = drawn.shape.index(max(drawn.shape))
    neighbour = place[:widest] + [(place[widest] + 1) % drawn.shape[widest]] + place[widest + 1:]
    return drawn.at[tuple(place)].set(smallest).at[tuple(neighbour)].set(top_value)


def block_levels(own_key, dims, shards, low, high):
    level = 1.0
    for axis_at, shards_of in shards:
        steps = jax.random.uniform(jax.random.fold_in(jax.random.fold_in(own_key, 6), axis_at), (shards_of,), jnp.float32, low / len(shards), high / len(shards))
        level = level * jnp.repeat(jnp.exp(steps), dims[axis_at] // shards_of).reshape((-1,) + (1,) * (len(dims) - 1 - axis_at))
    return level


def routed_block(key, own, number, rows, number_of, top, reach, lean):
    order = jax.random.permutation(key, number_of)
    packed, usual = shares(number_of, rows * top, reach, lean, True), shares(number_of, rows * top, reach, lean, False)
    places = jnp.arange(number_of)

    def named(lengths, rotation):
        used = int((lengths > 0).sum())
        fixed = max(1, used // 4)
        shifted = fixed + (places - fixed + rotation * (used - fixed)) % max(1, number_of - fixed)
        return jnp.zeros((number_of,), jnp.int32).at[order[jnp.where(places < fixed, places, shifted)]].set(jnp.asarray(lengths, jnp.int32))

    lengths = jnp.where(number % 4 == 0, named(packed, number // 4), named(usual, number - number // 4 - 1))
    mixed = jax.random.permutation(jax.random.fold_in(own, 3), number_of)
    giver, receiver = mixed[0:number_of // 2 * 2:2], mixed[1:number_of // 2 * 2:2]
    slack = jnp.minimum(lengths[giver] - 1, reach - lengths[receiver]) // 2
    slack = jnp.where((giver == order[0]) | (receiver == order[0]) | (lengths[receiver] == 0), 0, jnp.maximum(slack, 0))
    shifted = jax.random.randint(jax.random.fold_in(own, 4), (number_of // 2,), 0, 1 << 20) % (slack + 1)
    lengths = lengths.at[giver].add(-shifted).at[receiver].add(shifted)
    members = jnp.searchsorted(jnp.cumsum(lengths), jnp.arange(rows * top), side="right").astype(jnp.int32)
    grid = members.reshape(top, rows).T
    grid = grid[jax.random.permutation(jax.random.fold_in(own, 1), rows)]
    rotation = jax.random.randint(jax.random.fold_in(own, 2), (rows, 1), 0, top)
    return jnp.take_along_axis(grid, (jnp.arange(top)[None, :] + rotation) % top, axis=1)


def shares(count, total, limit, skew, full):
    portions = [(1 << 20) // math.isqrt(rank ** skew) + 1 for rank in range(1, count + 1)]
    largest = limit if full else min(limit, max(-(-total // count), total * portions[0] // sum(portions)))
    least = 1 if total - largest >= count - 1 else 0
    given, spare = [largest] + [least] * (count - 1), total - largest - least * (count - 1)
    while spare > 0:
        candidates = [i for i in range(1, count) if given[i] < largest] or [i for i in range(1, count) if given[i] < limit]
        pool, left = sum([portions[i] for i in candidates]), spare
        for i in candidates:
            addition = min(limit - given[i], max(1, left * portions[i] // pool), spare)
            given[i] = given[i] + addition
            spare = spare - addition
    return np.array(given)


def scatter_about(stream_key, dims, width, most, split=(), kind=jnp.bfloat16):
    factor_of = block_levels(stream_key, dims, split, -0.22, 0.18) if split else 1.0
    values = jax.random.normal(stream_key, dims, jnp.float32) * width * factor_of
    return jnp.minimum(jnp.maximum(values, -most), most).astype(kind)


def setup_inputs(seed: int = 0) -> dict:
    splits = jax.random.split(jax.random.key(seed), 14)
    positions = jnp.clip(1.0 * jax.random.uniform(splits[0], (3, FX, FY, 128), jnp.float32) ** block_levels(splits[0], (3, FX, FY, 128), ((1, 64), (2, 4)), -0.2, 0.2), 0.0, 1.0)
    pressure_start = jnp.clip(2.0 * jax.random.uniform(splits[1], (FX, FY, 128), jnp.float32) ** block_levels(splits[1], (FX, FY, 128), ((0, 64), (1, 4)), -0.2, 0.2), 0.0, 2.0)
    source = jnp.clip(jnp.exp(math.log(2.0) - 2.3025851 * jax.random.uniform(splits[2], (FX, FY, 128), jnp.float32) ** block_levels(splits[2], (FX, FY, 128), ((0, 64), (1, 4)), -0.2, 0.2)), 0.2, 2.0)
    resist = jnp.clip(jnp.exp(math.log(0.2) - 2.3025851 * jax.random.uniform(splits[3], (FX, FY, 128), jnp.float32) ** block_levels(splits[3], (FX, FY, 128), ((0, 64), (1, 4)), -0.2, 0.2)), 0.02, 0.2)
    neighbour_tiles = draw_neighbour_tiles(jax.random.fold_in(splits[13], 71), 0)
    pair_owner_keys = jax.random.split(jax.random.fold_in(splits[5], 1), PAIRS // CP)
    pair_owner_turns = jax.random.permutation(jax.random.fold_in(splits[5], 3), PAIRS // CP)
    pair_owner = jax.vmap(lambda own, number: routed_block(jax.random.fold_in(splits[5], 2), own, number, CP, N_BLK, 1, CAP, 2))(pair_owner_keys, pair_owner_turns).reshape((PAIRS, 1))
    pair_fluid = with_ends(jax.random.randint(splits[6], (PAIRS,), 0, TX * TY * 128), jax.random.fold_in(splits[6], 1), 0, (TX * TY * 128) - 1).astype(jnp.int32)
    pair_grain = with_ends(jax.random.randint(splits[7], (PAIRS,), 0, G_DEV), jax.random.fold_in(splits[7], 1), 0, G_DEV - 1).astype(jnp.int32)
    pair_normal = scatter_about(splits[8], (3, PAIRS), 1.0, 6.0, ((1, 256),), jnp.float32)
    grain_positions = jnp.clip(1.0 * jax.random.uniform(splits[9], (3, GRAINS), jnp.float32) ** block_levels(splits[9], (3, GRAINS), ((1, 256),), -0.2, 0.2), 0.0, 1.0)
    grain_velocity = scatter_about(splits[10], (3, GRAINS), 1.0, 6.0, ((1, 256),), jnp.float32)
    grain_mass = jnp.clip(jnp.exp(math.log(2.0) - 1.3862944 * jax.random.uniform(splits[11], (GRAINS,), jnp.float32) ** block_levels(splits[11], (GRAINS,), ((0, 256),), -0.2, 0.2)), 0.5, 2.0)
    contact_tiles = with_ends(jax.random.randint(splits[12], (GTILES, KG), 0, G_DEV // 128), jax.random.fold_in(splits[12], 1), 0, (G_DEV // 128) - 1).astype(jnp.int32)
    return {"positions": positions, "pressure_start": pressure_start, "source": source, "resist": resist, "neighbour_tiles": neighbour_tiles, "pair_owner": pair_owner, "pair_fluid": pair_fluid, "pair_grain": pair_grain, "pair_normal": pair_normal, "grain_positions": grain_positions, "grain_velocity": grain_velocity, "grain_mass": grain_mass, "contact_tiles": contact_tiles}


HIGH = lax.Precision.HIGHEST


def pair_sums(own, near_pos, near_val, scale):
    dist = jnp.zeros((own.shape[1], near_pos.shape[2], own.shape[2], near_pos.shape[3]), jnp.float32)
    for comp in range(3):
        delta = own[comp][:, None, :, None] - near_pos[comp][:, :, None, :]
        dist = dist + delta * delta
    weight = jnp.maximum(0.0, 1.0 - dist) ** 3 * (scale / (near_pos.shape[3] * near_pos.shape[2]))
    total = jnp.sum(weight, axis=(1, 3))
    applied = jnp.einsum("gkij,cgkj->cgi", weight, near_val, precision=HIGH)
    return total, applied


def blocked_sums(own, near_pos, near_val, scale, group):
    count = own.shape[1]

    def one_block(index):
        start = index * group
        return pair_sums(lax.dynamic_slice_in_dim(own, start, group, 1),
                         lax.dynamic_slice_in_dim(near_pos, start, group, 1),
                         lax.dynamic_slice_in_dim(near_val, start, group, 1), scale)

    total, applied = lax.map(one_block, jnp.arange(count // group, dtype=jnp.int32))
    return total.reshape(count, -1), jnp.moveaxis(applied, 0, 1).reshape(near_val.shape[0], count, -1)


def reference(positions, pressure_start, source, resist, neighbour_tiles, pair_owner, pair_fluid, pair_grain, pair_normal, grain_positions, grain_velocity, grain_mass, contact_tiles):
    base_x = (jnp.arange(FX, dtype=jnp.int32) // TX) * TX
    base_y = (jnp.arange(FY, dtype=jnp.int32) // TY) * TY
    ext_x = neighbour_tiles // (TY + 2)
    ext_y = neighbour_tiles % (TY + 2)
    near_index = ((base_x[:, None, None] + ext_x) * (FY + 2) + base_y[None, :, None] + ext_y).reshape(-1, KN)
    ext_pos = jnp.pad(positions, ((0, 0), (1, 1), (1, 1), (0, 0))).reshape(3, -1, 128)
    near_pos = ext_pos[:, near_index]
    own = positions.reshape(3, -1, 128)
    tiles = own.shape[1]
    group = math.gcd(64, tiles)
    press = pressure_start
    for step in range(ITERS):
        ext_press = jnp.pad(press, ((1, 1), (1, 1), (0, 0))).reshape(1, -1, 128)
        near_press = ext_press[:, near_index]
        total, applied = blocked_sums(own, near_pos, near_press, 1.0, group)
        press = ((source.reshape(-1, 128) + applied[0]) / (total + resist.reshape(-1, 128))).reshape(FX, FY, 128)
    device = jnp.arange(PAIRS, dtype=jnp.int32) // CP
    cross = device % N_CRS
    along = device // N_CRS
    tile = pair_fluid // 128
    fluid_index = ((along * TX + tile // TY) * FY + cross * TY + tile % TY) * 128 + pair_fluid % 128
    force = press.reshape(-1)[fluid_index][None, :] * pair_normal
    grain_index = (pair_owner[:, 0] * N_CRS + cross) * G_DEV + pair_grain
    coupling = jax.ops.segment_sum(force.T, grain_index, num_segments=GRAINS).T
    per_brick = G_DEV // 128
    brick = jnp.arange(GTILES, dtype=jnp.int32) // per_brick
    contact_index = brick[:, None] * per_brick + contact_tiles
    grain_pos = grain_positions.reshape(3, GTILES, 128)
    grain_vel = grain_velocity.reshape(3, GTILES, 128)
    total, applied = blocked_sums(grain_pos, grain_pos[:, contact_index], grain_vel[:, contact_index], 4.0, math.gcd(64, GTILES))
    contact = applied - total[None] * grain_vel
    grain_new = grain_vel + 0.1 * (coupling.reshape(3, GTILES, 128) + contact) / grain_mass.reshape(GTILES, 128)
    grain_new = grain_new.reshape(3, GRAINS)
    return press, grain_new, grain_new[:, grain_index]
```

```python
import jax
import jax.numpy as jnp
from jax import lax
from jax.experimental import pallas as pl
from jax.experimental.pallas import tpu as pltpu
from jax.sharding import PartitionSpec as P

TX, TY, L, KN, ITERS = 16, 8, 128, 6, 3
HALO = ITERS
EX = TX + 2 * HALO
EY = 16
TILES = EX * EY
PLANES = 7
K = 32
CAP = 64
F32, BF16, I32 = jnp.float32, jnp.bfloat16, jnp.int32
NT = (((1,), (1,)), ((), ()))
NN = (((1,), (0,)), ((), ()))
TN = (((0,), (0,)), ((), ()))


def dot(a, b, dims):
    return lax.dot_general(a, b, dims, preferred_element_type=F32)


def split3(x):
    high = x.astype(BF16).astype(F32)
    rest = x - high
    mid = rest.astype(BF16).astype(F32)
    return high, mid, rest - mid


def iota(shape, dim):
    return lax.broadcasted_iota(I32, shape, dim)


def distance_rows(xyz):
    left, right = [], []
    for comp in xyz:
        h, m, l = split3(comp)
        left += [2 * h, 2 * m, 2 * h, 2 * l, 2 * h, 2 * m]
        right += [h, h, m, h, l, m]
    norm = xyz[0] * xyz[0] + xyz[1] * xyz[1] + xyz[2] * xyz[2]
    one = jnp.ones_like(norm)
    left += list(split3(1.0 - norm)) + [one] * 3
    right += [one] * 3 + list(split3(-norm))
    return left, right


def store_rows(stage, rows, first, count):
    for k, row in enumerate(rows):
        stage[pl.ds(first * K + k, count, stride=K), :] = row


def cube(t):
    w = jnp.maximum(t, 0.0)
    return w * w * w


def column_sum(acc):
    return jnp.sum(acc.T, axis=0, keepdims=True)


def prep_kernel(contact_ref, owner_ref, pos_ref, vel_ref, mass_ref, rank_ref, base_ref, gain_ref, stage_a, stage_b):
    owner = owner_ref[...]
    upper = (iota((256, 256), 0) < iota((256, 256), 1)).astype(BF16)
    every = jnp.ones((256, 256), BF16)
    carry = jnp.zeros((64, 256), F32)
    for q in range(0, owner.shape[1], 256):
        named = iota((64, 256), 0) == owner[:, q : q + 256]
        hot = named.astype(F32).astype(BF16)
        before = dot(hot, upper, NN) + carry
        rank_ref[:, q : q + 256] = jnp.sum(jnp.where(named, before, 0.0), axis=0, keepdims=True).astype(I32)
        carry = carry + dot(hot, every, NN)
    tiles = vel_ref.shape[1]
    stage_a[...] = jnp.zeros_like(stage_a)
    stage_b[...] = jnp.zeros_like(stage_b)
    left, right = distance_rows([pos_ref[c] for c in range(3)])
    store_rows(stage_a, left, 0, tiles)
    store_rows(stage_b, right, 0, tiles)
    gain = 0.1 / mass_ref[...]
    gain_ref[...] = gain
    for t in range(tiles):
        a = stage_a[t * K : (t + 1) * K, :].astype(BF16)
        total = jnp.zeros((L, L), F32)
        applied = [jnp.zeros((L, L), F32) for _ in range(3)]
        for k in range(4):
            n = contact_ref[t * 4 + k]
            b = stage_b[pl.ds(pl.multiple_of(n * K, K), K), :].astype(BF16)
            w = cube(dot(a, b, TN))
            total = total + w
            for c in range(3):
                applied[c] = applied[c] + w * vel_ref[c, pl.ds(n, 1), :]
        total = column_sum(total)
        for c in range(3):
            own = vel_ref[c, t : t + 1, :]
            contact = (column_sum(applied[c]) - total * own) * (4.0 / 512)
            base_ref[c, t : t + 1, :] = own + gain[t : t + 1, :] * contact


def fluid_kernel(
    own_pos, own_press, own_src, own_res, own_dir, ylow, yhigh, xlow, xhigh, owner_ref, rank_ref, fluid_ref, grain_ref, normal_ref,
    press_ref, send_ref,
    ext, near_v, near_s, stage, left_s, right_s, num_s, deg_s, sem,
):
    blk, crs = lax.axis_index("blk"), lax.axis_index("crs")
    blks, crss = lax.axis_size("blk"), lax.axis_size("crs")
    ext[:, HALO * EY : (HALO + TX) * EY, :] = jnp.zeros((PLANES, TX * EY, L), F32)
    for x in range(HALO):
        for p in range(PLANES):
            ext[p, x * EY : (x + 1) * EY, :] = xlow[p, x]
            ext[p, (HALO + TX + x) * EY : (HALO + TX + x + 1) * EY, :] = xhigh[p, x]
    for x in range(TX):
        r = (HALO + x) * EY
        for p, plane in enumerate((own_pos.at[0], own_pos.at[1], own_pos.at[2], own_press, own_src, own_res, own_dir)):
            ext[p, r : r + TY, :] = plane[x]
            ext[p, r + TY : r + TY + HALO, :] = yhigh[p, x]
            ext[p, r + EY - HALO : r + EY, :] = ylow[p, x]
    stage[...] = jnp.zeros_like(stage)

    def build(ex, _):
        r = pl.multiple_of(ex * EY, EY)
        way = ext[6, pl.ds(r, EY), :].astype(I32)
        dx = lax.shift_right_logical(way * 11, 5)
        dy = way - 3 * dx - 1
        near_v[pl.ds(r, EY), :] = (ex + dx - 1) * EY + ((iota((EY, L), 0) + dy) & (EY - 1))
        left, right = distance_rows([ext[c, pl.ds(r, EY), :] for c in range(3)])
        for rows, target in ((left, left_s), (right, right_s)):
            for half in range(0, EY, 8):
                store_rows(stage, [row[half : half + 8] for row in rows], half, 8)
            target[pl.ds(pl.multiple_of(r * K, EY * K), EY * K), :] = stage[...].astype(BF16)
        return 0

    lax.fori_loop(0, EX, build, 0)
    copy = pltpu.make_async_copy(near_v, near_s, sem)
    copy.start()
    copy.wait()

    def one_tile(t, with_deg):
        a = left_s[pl.ds(pl.multiple_of(t * K, K), K), :]
        acc = jnp.zeros((L, L), F32)
        tot = jnp.zeros((L, L), F32)
        for k in range(0, KN, 2):
            n = [near_s[t, k + e] for e in range(2)]
            b = jnp.concatenate([right_s[pl.ds(pl.multiple_of(m * K, K), K), :] for m in n], axis=1)
            w = cube(dot(a, b, TN))
            for e in range(2):
                part = w[:, e * L : (e + 1) * L]
                acc = acc + part * ext[3, pl.ds(n[e], 1), :]
                if with_deg:
                    tot = tot + part
        num_s[pl.ds(t, 1), :] = column_sum(acc)
        if with_deg:
            deg_s[pl.ds(t, 1), :] = column_sum(tot)

    for step in range(ITERS):
        ring = ITERS - 1 - step
        pairs = (TY + 2 * ring) // 2

        def row(x, _):
            def two(j, _):
                for e in range(2):
                    y = 2 * j + e + EY - ring
                    one_tile(x * EY + (y & (EY - 1)), step == 0)
                return 0

            return lax.fori_loop(0, pairs, two, 0)

        lax.fori_loop(HALO - ring, HALO + TX + ring, row, 0)

        def divide(x, _):
            r = pl.multiple_of(x * EY, EY)
            rows = pl.ds(r, EY)
            y = iota((EY, L), 0)
            y = jnp.where(y >= EY - HALO, y - EY, y)
            gy = y + crs * TY
            gx = x - HALO + blk * TX
            inside = (gy >= 0) & (gy < crss * TY) & (gx >= 0) & (gx < blks * TX)
            scale = 1.0 / (KN * L)
            new = (ext[4, rows, :] + num_s[rows, :] * scale) / (deg_s[rows, :] * scale + ext[5, rows, :])
            ext[3, rows, :] = jnp.where(inside, new, 0.0)
            return 0

        lax.fori_loop(HALO - ring, HALO + TX + ring, divide, 0)
    for x in range(TX):
        press_ref[x] = ext[3, (HALO + x) * EY : (HALO + x) * EY + TY, :]
    press = press_ref[...].reshape(TX * TY, L)
    parts = jnp.concatenate([s.astype(BF16) for s in split3(press)], axis=1)
    total01 = jnp.zeros((64, L), F32)
    total23 = jnp.zeros((64, L), F32)
    chunk = 512
    for q in range(0, owner_ref.shape[1], chunk):
        cols = slice(q, q + chunk)
        fluid = fluid_ref[:, cols]
        lane = (iota((L, chunk), 0) == (fluid & (L - 1))).astype(F32).astype(BF16)
        found = dot(parts, jnp.concatenate([lane] * 3, axis=0), NN)
        tile = iota((TX * TY, chunk), 0) == lax.shift_right_logical(fluid, 7)
        at = jnp.sum(jnp.where(tile, found, 0.0), axis=0, keepdims=True)
        owned = iota((64, chunk), 0) == owner_ref[:, cols]
        slot = iota((L, chunk), 0)
        rank = rank_ref[:, cols]
        low = (slot == rank).astype(F32).astype(BF16)
        high = (slot == rank + CAP).astype(F32).astype(BF16)
        rows = [at * normal_ref[c : c + 1, cols] for c in range(3)] + [grain_ref[:, cols].astype(F32)]

        def spread(pair):
            out = jnp.zeros((64, L), F32)
            for value, hot in zip(pair, (low, high)):
                for part in split3(value):
                    out = out + dot(jnp.where(owned, part, 0.0).astype(BF16), hot, NT)
            return out

        total01 = total01 + spread(rows[:2])
        total23 = total23 + spread(rows[2:])
    send_ref[:, :L] = total01
    send_ref[:, L:] = total23


def grain_kernel(got_ref, base_ref, gain_ref, new_ref, back_ref):
    count = got_ref.shape[1]
    grain = got_ref[3:4, :].astype(I32)
    tile = iota((8, count), 0) == lax.shift_right_logical(grain, 7)
    lane = (iota((L, count), 0) == (grain & (L - 1))).astype(F32).astype(BF16)
    rows = []
    for c in range(3):
        for part in split3(got_ref[c : c + 1, :]):
            rows.append(jnp.where(tile, part, 0.0))
    summed = dot(jnp.concatenate(rows, axis=0).astype(BF16), lane, NT)
    new = []
    for c in range(3):
        coupling = summed[c * 24 : c * 24 + 8] + summed[c * 24 + 8 : c * 24 + 16] + summed[c * 24 + 16 : c * 24 + 24]
        new.append(base_ref[c] + gain_ref[...] * coupling)
        for g in range(8):
            new_ref[c : c + 1, g * L : (g + 1) * L] = new[c][g : g + 1]
    parts = jnp.concatenate([s.astype(BF16) for s in split3(jnp.concatenate(new, axis=0))], axis=1)
    found = dot(parts, jnp.concatenate([lane] * 3, axis=0), NN)
    for c in range(3):
        back_ref[c : c + 1, :] = jnp.sum(jnp.where(tile, found[c * 8 : c * 8 + 8], 0.0), axis=0, keepdims=True)


def pick_kernel(got_ref, owner_ref, rank_ref, out_ref):
    blocks = jnp.concatenate([got_ref[:, c * CAP : (c + 1) * CAP] for c in range(3)], axis=0)
    parts = [s.astype(BF16) for s in split3(blocks)]
    chunk = 512
    for q in range(0, owner_ref.shape[1], chunk):
        cols = slice(q, q + chunk)
        slot = (iota((CAP, chunk), 0) == rank_ref[:, cols]).astype(F32).astype(BF16)
        found = dot(parts[0], slot, NN) + dot(parts[1], slot, NN) + dot(parts[2], slot, NN)
        owned = iota((64, chunk), 0) == owner_ref[:, cols]
        for c in range(3):
            out_ref[c : c + 1, cols] = jnp.sum(jnp.where(owned, found[c * 64 : (c + 1) * 64], 0.0), axis=0, keepdims=True)


VMEM = pl.BlockSpec(memory_space=pltpu.VMEM)
SMEM = pl.BlockSpec(memory_space=pltpu.SMEM)


def shape(*dims, dtype=F32):
    return jax.ShapeDtypeStruct(dims, dtype)


def cost(flops, size):
    return pl.CostEstimate(flops=flops, bytes_accessed=size, transcendentals=0)


def shifts(axis):
    count = lax.axis_size(axis)
    forward = [(i, i + 1) for i in range(count - 1)]
    return forward, [(b, a) for a, b in forward]


def on_device(positions, pressure_start, source, resist, neighbour_tiles, pair_owner, pair_fluid, pair_grain, pair_normal,
              grain_positions, grain_velocity, grain_mass, contact_tiles):
    pairs = pair_fluid.shape[0]
    owner = pair_owner.reshape(1, pairs)
    fluid = pair_fluid.reshape(1, pairs)
    grain = pair_grain.reshape(1, pairs)
    here_x = jnp.arange(TX, dtype=I32)[:, None, None]
    here_y = jnp.arange(TY, dtype=I32)[None, :, None]
    way = (neighbour_tiles // (TY + 2) - here_x) * 3 + neighbour_tiles % (TY + 2) - here_y
    way = jnp.pad(way.astype(F32), ((0, 0), (0, 0), (0, L - KN)))

    def planes(xs, ys):
        return jnp.concatenate(
            [positions[:, xs, ys], pressure_start[None, xs, ys], source[None, xs, ys], resist[None, xs, ys], way[None, xs, ys]], axis=0
        )

    every, first, last = slice(None), slice(0, HALO), slice(-HALO, None)
    forward, backward = shifts("crs")
    ylow = lax.ppermute(planes(every, last), "crs", forward)
    yhigh = lax.ppermute(planes(every, first), "crs", backward)
    gap = jnp.zeros((PLANES, HALO, EY - TY - 2 * HALO, L), F32)

    def wide(xs):
        return jnp.concatenate([planes(xs, every), yhigh[:, xs], gap, ylow[:, xs]], axis=2)

    forward, backward = shifts("blk")
    xlow = lax.ppermute(wide(last), "blk", forward)
    xhigh = lax.ppermute(wide(first), "blk", backward)

    grain_tiles = grain_mass.shape[0] // L
    rank, base, gain = pl.pallas_call(
        prep_kernel,
        out_shape=(shape(1, pairs, dtype=I32), shape(3, grain_tiles, L), shape(grain_tiles, L)),
        in_specs=[SMEM] + [VMEM] * 4,
        out_specs=(VMEM,) * 3,
        scratch_shapes=[pltpu.VMEM((grain_tiles * K, L), F32)] * 2,
        compiler_params=pltpu.CompilerParams(vmem_limit_bytes=32 << 20),
        cost_estimate=cost(10**9, 10**6),
        name="prep",
    )(contact_tiles.reshape(-1), owner, grain_positions.reshape(3, grain_tiles, L), grain_velocity.reshape(3, grain_tiles, L), grain_mass.reshape(grain_tiles, L))

    press, send = pl.pallas_call(
        fluid_kernel,
        out_shape=(shape(TX, TY, L), shape(64, 4 * CAP)),
        in_specs=[VMEM] * 14,
        out_specs=(VMEM,) * 2,
        scratch_shapes=[
            pltpu.VMEM((PLANES, TILES, L), F32),
            pltpu.VMEM((TILES, L), I32),
            pltpu.SMEM((TILES, L), I32),
            pltpu.VMEM((EY * K, L), F32),
            pltpu.VMEM((TILES * K, L), BF16),
            pltpu.VMEM((TILES * K, L), BF16),
            pltpu.VMEM((TILES, L), F32),
            pltpu.VMEM((TILES, L), F32),
            pltpu.SemaphoreType.DMA,
        ],
        compiler_params=pltpu.CompilerParams(vmem_limit_bytes=32 << 20),
        cost_estimate=cost(10**10, 10**7),
        name="fluid",
    )(positions, pressure_start, source, resist, way, ylow, yhigh, xlow, xhigh, owner, rank, fluid, grain, pair_normal)

    got = lax.all_to_all(send, "blk", 0, 0, tiled=True)
    got = got.reshape(64, 4, CAP).swapaxes(0, 1).reshape(4, 64 * CAP)
    grain_new, back = pl.pallas_call(
        grain_kernel,
        out_shape=(shape(3, grain_tiles * L), shape(3, 64 * CAP)),
        in_specs=[VMEM] * 3,
        out_specs=(VMEM,) * 2,
        compiler_params=pltpu.CompilerParams(vmem_limit_bytes=32 << 20),
        cost_estimate=cost(10**9, 10**6),
        name="grain",
    )(got, base, gain)
    back = back.reshape(3, 64, CAP).swapaxes(0, 1).reshape(64, 3 * CAP)
    seen = lax.all_to_all(back, "blk", 0, 0, tiled=True)
    seen = pl.pallas_call(
        pick_kernel,
        out_shape=shape(3, pairs),
        in_specs=[VMEM] * 3,
        out_specs=VMEM,
        compiler_params=pltpu.CompilerParams(vmem_limit_bytes=32 << 20),
        cost_estimate=cost(10**9, 10**6),
        name="pick",
    )(seen, owner, rank)
    return press, grain_new, seen


def solution(mesh):
    in_specs = (
        P(None, "blk", "crs", None),
        P("blk", "crs", None),
        P("blk", "crs", None),
        P("blk", "crs", None),
        P("blk", "crs", None),
        P(("blk", "crs"), None),
        P(("blk", "crs")),
        P(("blk", "crs")),
        P(None, ("blk", "crs")),
        P(None, ("blk", "crs")),
        P(None, ("blk", "crs")),
        P(("blk", "crs")),
        P(("blk", "crs"), None),
    )
    out_specs = (P("blk", "crs", None), P(None, ("blk", "crs")), P(None, ("blk", "crs")))
    return jax.shard_map(on_device, mesh=mesh, in_specs=in_specs, out_specs=out_specs, check_vma=False)
```

```python
import jax
import jax.numpy as jnp
from jax import lax
from jax.experimental import pallas as pl
from jax.experimental.pallas import tpu as pltpu
from jax.sharding import PartitionSpec as P

TX, TY, L, KN, ITERS = 16, 8, 128, 6, 3
HALO = ITERS
EX = TX + 2 * HALO
EY = 16
TILES = EX * EY
PLANES = 7
K = 32
CAP = 64
F32, BF16, I32 = jnp.float32, jnp.bfloat16, jnp.int32
NT = (((1,), (1,)), ((), ()))
NN = (((1,), (0,)), ((), ()))
TN = (((0,), (0,)), ((), ()))


def dot(a, b, dims):
    return lax.dot_general(a, b, dims, preferred_element_type=F32)


def split3(x):
    high = x.astype(BF16).astype(F32)
    rest = x - high
    mid = rest.astype(BF16).astype(F32)
    return high, mid, rest - mid


def iota(shape, dim):
    return lax.broadcasted_iota(I32, shape, dim)


def distance_rows(xyz):
    left, right = [], []
    for comp in xyz:
        h, m, l = split3(comp)
        left += [2 * h, 2 * m, 2 * h, 2 * l, 2 * h, 2 * m]
        right += [h, h, m, h, l, m]
    norm = xyz[0] * xyz[0] + xyz[1] * xyz[1] + xyz[2] * xyz[2]
    one = jnp.ones_like(norm)
    left += list(split3(1.0 - norm)) + [one] * 3
    right += [one] * 3 + list(split3(-norm))
    return left, right


def store_rows(stage, rows, first, count):
    for k, row in enumerate(rows):
        stage[pl.ds(first * K + k, count, stride=K), :] = row


def cube(t):
    w = jnp.maximum(t, 0.0)
    return w * w * w


def column_sum(acc):
    return jnp.sum(acc.T, axis=0, keepdims=True)


def prep_kernel(contact_ref, owner_ref, pos_ref, vel_ref, mass_ref, rank_ref, base_ref, gain_ref, stage_a, stage_b):
    owner = owner_ref[...]
    upper = (iota((256, 256), 0) < iota((256, 256), 1)).astype(BF16)
    every = jnp.ones((256, 256), BF16)
    carry = jnp.zeros((64, 256), F32)
    for q in range(0, owner.shape[1], 256):
        named = iota((64, 256), 0) == owner[:, q : q + 256]
        hot = named.astype(F32).astype(BF16)
        before = dot(hot, upper, NN) + carry
        rank_ref[:, q : q + 256] = jnp.sum(jnp.where(named, before, 0.0), axis=0, keepdims=True).astype(I32)
        carry = carry + dot(hot, every, NN)
    tiles = vel_ref.shape[1]
    stage_a[...] = jnp.zeros_like(stage_a)
    stage_b[...] = jnp.zeros_like(stage_b)
    left, right = distance_rows([pos_ref[c] for c in range(3)])
    store_rows(stage_a, left, 0, tiles)
    store_rows(stage_b, right, 0, tiles)
    gain = 0.1 / mass_ref[...]
    gain_ref[...] = gain
    for t in range(tiles):
        a = stage_a[t * K : (t + 1) * K, :].astype(BF16)
        total = jnp.zeros((L, L), F32)
        applied = [jnp.zeros((L, L), F32) for _ in range(3)]
        for k in range(4):
            n = contact_ref[t * 4 + k]
            b = stage_b[pl.ds(pl.multiple_of(n * K, K), K), :].astype(BF16)
            w = cube(dot(a, b, TN))
            total = total + w
            for c in range(3):
                applied[c] = applied[c] + w * vel_ref[c, pl.ds(n, 1), :]
        total = column_sum(total)
        for c in range(3):
            own = vel_ref[c, t : t + 1, :]
            contact = (column_sum(applied[c]) - total * own) * (4.0 / 512)
            base_ref[c, t : t + 1, :] = own + gain[t : t + 1, :] * contact


def fluid_kernel(
    own_pos, own_press, own_src, own_res, own_dir, ylow, yhigh, xlow, xhigh, owner_ref, rank_ref, fluid_ref, grain_ref, normal_ref,
    press_ref, send_ref,
    ext, near_v, near_s, stage, left_s, right_s, num_s, deg_s, kept, sem,
):
    blk, crs = lax.axis_index("blk"), lax.axis_index("crs")
    blks, crss = lax.axis_size("blk"), lax.axis_size("crs")
    ext[:, HALO * EY : (HALO + TX) * EY, :] = jnp.zeros((PLANES, TX * EY, L), F32)
    for x in range(HALO):
        for p in range(PLANES):
            ext[p, x * EY : (x + 1) * EY, :] = xlow[p, x]
            ext[p, (HALO + TX + x) * EY : (HALO + TX + x + 1) * EY, :] = xhigh[p, x]
    for x in range(TX):
        r = (HALO + x) * EY
        for p, plane in enumerate((own_pos.at[0], own_pos.at[1], own_pos.at[2], own_press, own_src, own_res, own_dir)):
            ext[p, r : r + TY, :] = plane[x]
            ext[p, r + TY : r + TY + HALO, :] = yhigh[p, x]
            ext[p, r + EY - HALO : r + EY, :] = ylow[p, x]
    stage[...] = jnp.zeros_like(stage)

    def build(ex, _):
        r = pl.multiple_of(ex * EY, EY)
        way = ext[6, pl.ds(r, EY), :].astype(I32)
        dx = lax.shift_right_logical(way * 11, 5)
        dy = way - 3 * dx - 1
        near_v[pl.ds(r, EY), :] = (ex + dx - 1) * EY + ((iota((EY, L), 0) + dy) & (EY - 1))
        left, right = distance_rows([ext[c, pl.ds(r, EY), :] for c in range(3)])
        for rows, target in ((left, left_s), (right, right_s)):
            for half in range(0, EY, 8):
                store_rows(stage, [row[half : half + 8] for row in rows], half, 8)
            target[pl.ds(pl.multiple_of(r * K, EY * K), EY * K), :] = stage[...].astype(BF16)
        return 0

    lax.fori_loop(0, EX, build, 0)
    copy = pltpu.make_async_copy(near_v, near_s, sem)
    copy.start()
    copy.wait()

    def one_tile(t, with_deg, slot=None):
        a = left_s[pl.ds(pl.multiple_of(t * K, K), K), :]
        acc = jnp.zeros((L, L), F32)
        tot = jnp.zeros((L, L), F32)
        for k in range(0, KN, 2):
            n = [near_s[t, k + e] for e in range(2)]
            b = jnp.concatenate([right_s[pl.ds(pl.multiple_of(m * K, K), K), :] for m in n], axis=1)
            w = cube(dot(a, b, TN))
            for e in range(2):
                part = w[:, e * L : (e + 1) * L]
                if slot is not None:
                    kept[slot, k + e] = part
                acc = acc + part * ext[3, pl.ds(n[e], 1), :]
                if with_deg:
                    tot = tot + part
        num_s[pl.ds(t, 1), :] = column_sum(acc)
        if with_deg:
            deg_s[pl.ds(t, 1), :] = column_sum(tot)

    def kept_tile(t, slot):
        acc = jnp.zeros((L, L), F32)
        for k in range(KN):
            acc = acc + kept[slot, k] * ext[3, pl.ds(near_s[t, k], 1), :]
        num_s[pl.ds(t, 1), :] = column_sum(acc)

    for step in range(ITERS):
        ring = ITERS - 1 - step

        def outer_row(i, _):
            x = HALO - ring + i + jnp.where(i >= ring, TX, 0)
            for y in range(-ring, TY + ring):
                one_tile(x * EY + y % EY, step == 0)
            return 0

        def own_row(i, _):
            for y in range(-ring, TY + ring):
                t = (i + HALO) * EY + y % EY
                if y < 0 or y >= TY:
                    one_tile(t, step == 0)
                elif step == 0:
                    one_tile(t, True, i * TY + y)
                else:
                    kept_tile(t, i * TY + y)
            return 0

        def own_rows(i, _):
            own_row(2 * i, 0)
            return own_row(2 * i + 1, 0)

        if ring:
            lax.fori_loop(0, 2 * ring, outer_row, 0)
            lax.fori_loop(0, TX, own_row, 0)
        else:
            lax.fori_loop(0, TX // 2, own_rows, 0)

        def divide(x, _):
            r = pl.multiple_of(x * EY, EY)
            rows = pl.ds(r, EY)
            y = iota((EY, L), 0)
            y = jnp.where(y >= EY - HALO, y - EY, y)
            gy = y + crs * TY
            gx = x - HALO + blk * TX
            inside = (gy >= 0) & (gy < crss * TY) & (gx >= 0) & (gx < blks * TX)
            scale = 1.0 / (KN * L)
            new = (ext[4, rows, :] + num_s[rows, :] * scale) / (deg_s[rows, :] * scale + ext[5, rows, :])
            ext[3, rows, :] = jnp.where(inside, new, 0.0)
            return 0

        lax.fori_loop(HALO - ring, HALO + TX + ring, divide, 0)
    for x in range(TX):
        press_ref[x] = ext[3, (HALO + x) * EY : (HALO + x) * EY + TY, :]
    press = press_ref[...].reshape(TX * TY, L)
    parts = jnp.concatenate([s.astype(BF16) for s in split3(press)], axis=1)
    total01 = jnp.zeros((64, L), F32)
    total23 = jnp.zeros((64, L), F32)
    chunk = 512
    for q in range(0, owner_ref.shape[1], chunk):
        cols = slice(q, q + chunk)
        fluid = fluid_ref[:, cols]
        lane = (iota((L, chunk), 0) == (fluid & (L - 1))).astype(F32).astype(BF16)
        found = dot(parts, jnp.concatenate([lane] * 3, axis=0), NN)
        tile = iota((TX * TY, chunk), 0) == lax.shift_right_logical(fluid, 7)
        at = jnp.sum(jnp.where(tile, found, 0.0), axis=0, keepdims=True)
        owned = iota((64, chunk), 0) == owner_ref[:, cols]
        slot = iota((L, chunk), 0)
        rank = rank_ref[:, cols]
        low = (slot == rank).astype(F32).astype(BF16)
        high = (slot == rank + CAP).astype(F32).astype(BF16)
        rows = [at * normal_ref[c : c + 1, cols] for c in range(3)] + [grain_ref[:, cols].astype(F32)]

        def spread(pair):
            out = jnp.zeros((64, L), F32)
            for value, hot in zip(pair, (low, high)):
                for part in split3(value):
                    out = out + dot(jnp.where(owned, part, 0.0).astype(BF16), hot, NT)
            return out

        total01 = total01 + spread(rows[:2])
        total23 = total23 + spread(rows[2:])
    send_ref[:, :L] = total01
    send_ref[:, L:] = total23


def grain_kernel(got_ref, base_ref, gain_ref, new_ref, back_ref):
    count = got_ref.shape[1]
    grain = got_ref[3:4, :].astype(I32)
    tile = iota((8, count), 0) == lax.shift_right_logical(grain, 7)
    lane = (iota((L, count), 0) == (grain & (L - 1))).astype(F32).astype(BF16)
    rows = []
    for c in range(3):
        for part in split3(got_ref[c : c + 1, :]):
            rows.append(jnp.where(tile, part, 0.0))
    summed = dot(jnp.concatenate(rows, axis=0).astype(BF16), lane, NT)
    new = []
    for c in range(3):
        coupling = summed[c * 24 : c * 24 + 8] + summed[c * 24 + 8 : c * 24 + 16] + summed[c * 24 + 16 : c * 24 + 24]
        new.append(base_ref[c] + gain_ref[...] * coupling)
        for g in range(8):
            new_ref[c : c + 1, g * L : (g + 1) * L] = new[c][g : g + 1]
    parts = jnp.concatenate([s.astype(BF16) for s in split3(jnp.concatenate(new, axis=0))], axis=1)
    found = dot(parts, jnp.concatenate([lane] * 3, axis=0), NN)
    for c in range(3):
        back_ref[c : c + 1, :] = jnp.sum(jnp.where(tile, found[c * 8 : c * 8 + 8], 0.0), axis=0, keepdims=True)


def pick_kernel(got_ref, owner_ref, rank_ref, out_ref):
    blocks = jnp.concatenate([got_ref[:, c * CAP : (c + 1) * CAP] for c in range(3)], axis=0)
    parts = [s.astype(BF16) for s in split3(blocks)]
    chunk = 512
    for q in range(0, owner_ref.shape[1], chunk):
        cols = slice(q, q + chunk)
        slot = (iota((CAP, chunk), 0) == rank_ref[:, cols]).astype(F32).astype(BF16)
        found = dot(parts[0], slot, NN) + dot(parts[1], slot, NN) + dot(parts[2], slot, NN)
        owned = iota((64, chunk), 0) == owner_ref[:, cols]
        for c in range(3):
            out_ref[c : c + 1, cols] = jnp.sum(jnp.where(owned, found[c * 64 : (c + 1) * 64], 0.0), axis=0, keepdims=True)


VMEM = pl.BlockSpec(memory_space=pltpu.VMEM)
SMEM = pl.BlockSpec(memory_space=pltpu.SMEM)


def shape(*dims, dtype=F32):
    return jax.ShapeDtypeStruct(dims, dtype)


def cost(flops, size):
    return pl.CostEstimate(flops=flops, bytes_accessed=size, transcendentals=0)


def shifts(axis):
    count = lax.axis_size(axis)
    forward = [(i, i + 1) for i in range(count - 1)]
    return forward, [(b, a) for a, b in forward]


def on_device(positions, pressure_start, source, resist, neighbour_tiles, pair_owner, pair_fluid, pair_grain, pair_normal,
              grain_positions, grain_velocity, grain_mass, contact_tiles):
    pairs = pair_fluid.shape[0]
    owner = pair_owner.reshape(1, pairs)
    fluid = pair_fluid.reshape(1, pairs)
    grain = pair_grain.reshape(1, pairs)
    here_x = jnp.arange(TX, dtype=I32)[:, None, None]
    here_y = jnp.arange(TY, dtype=I32)[None, :, None]
    way = (neighbour_tiles // (TY + 2) - here_x) * 3 + neighbour_tiles % (TY + 2) - here_y
    way = jnp.pad(way.astype(F32), ((0, 0), (0, 0), (0, L - KN)))

    def planes(xs, ys):
        return jnp.concatenate(
            [positions[:, xs, ys], pressure_start[None, xs, ys], source[None, xs, ys], resist[None, xs, ys], way[None, xs, ys]], axis=0
        )

    every, first, last = slice(None), slice(0, HALO), slice(-HALO, None)
    forward, backward = shifts("crs")
    ylow = lax.ppermute(planes(every, last), "crs", forward)
    yhigh = lax.ppermute(planes(every, first), "crs", backward)
    gap = jnp.zeros((PLANES, HALO, EY - TY - 2 * HALO, L), F32)

    def wide(xs):
        return jnp.concatenate([planes(xs, every), yhigh[:, xs], gap, ylow[:, xs]], axis=2)

    forward, backward = shifts("blk")
    xlow = lax.ppermute(wide(last), "blk", forward)
    xhigh = lax.ppermute(wide(first), "blk", backward)

    grain_tiles = grain_mass.shape[0] // L
    rank, base, gain = pl.pallas_call(
        prep_kernel,
        out_shape=(shape(1, pairs, dtype=I32), shape(3, grain_tiles, L), shape(grain_tiles, L)),
        in_specs=[SMEM] + [VMEM] * 4,
        out_specs=(VMEM,) * 3,
        scratch_shapes=[pltpu.VMEM((grain_tiles * K, L), F32)] * 2,
        compiler_params=pltpu.CompilerParams(vmem_limit_bytes=32 << 20),
        cost_estimate=cost(10**9, 10**6),
        name="prep",
    )(contact_tiles.reshape(-1), owner, grain_positions.reshape(3, grain_tiles, L), grain_velocity.reshape(3, grain_tiles, L), grain_mass.reshape(grain_tiles, L))

    press, send = pl.pallas_call(
        fluid_kernel,
        out_shape=(shape(TX, TY, L), shape(64, 4 * CAP)),
        in_specs=[VMEM] * 14,
        out_specs=(VMEM,) * 2,
        scratch_shapes=[
            pltpu.VMEM((PLANES, TILES, L), F32),
            pltpu.VMEM((TILES, L), I32),
            pltpu.SMEM((TILES, L), I32),
            pltpu.VMEM((EY * K, L), F32),
            pltpu.VMEM((TILES * K, L), BF16),
            pltpu.VMEM((TILES * K, L), BF16),
            pltpu.VMEM((TILES, L), F32),
            pltpu.VMEM((TILES, L), F32),
            pltpu.VMEM((TX * TY, KN, L, L), F32),
            pltpu.SemaphoreType.DMA,
        ],
        compiler_params=pltpu.CompilerParams(vmem_limit_bytes=60 << 20),
        cost_estimate=cost(10**10, 10**7),
        name="fluid",
    )(positions, pressure_start, source, resist, way, ylow, yhigh, xlow, xhigh, owner, rank, fluid, grain, pair_normal)

    got = lax.all_to_all(send, "blk", 0, 0, tiled=True)
    got = got.reshape(64, 4, CAP).swapaxes(0, 1).reshape(4, 64 * CAP)
    grain_new, back = pl.pallas_call(
        grain_kernel,
        out_shape=(shape(3, grain_tiles * L), shape(3, 64 * CAP)),
        in_specs=[VMEM] * 3,
        out_specs=(VMEM,) * 2,
        compiler_params=pltpu.CompilerParams(vmem_limit_bytes=32 << 20),
        cost_estimate=cost(10**9, 10**6),
        name="grain",
    )(got, base, gain)
    back = back.reshape(3, 64, CAP).swapaxes(0, 1).reshape(64, 3 * CAP)
    seen = lax.all_to_all(back, "blk", 0, 0, tiled=True)
    seen = pl.pallas_call(
        pick_kernel,
        out_shape=shape(3, pairs),
        in_specs=[VMEM] * 3,
        out_specs=VMEM,
        compiler_params=pltpu.CompilerParams(vmem_limit_bytes=32 << 20),
        cost_estimate=cost(10**9, 10**6),
        name="pick",
    )(seen, owner, rank)
    return press, grain_new, seen


def solution(mesh):
    in_specs = (
        P(None, "blk", "crs", None),
        P("blk", "crs", None),
        P("blk", "crs", None),
        P("blk", "crs", None),
        P("blk", "crs", None),
        P(("blk", "crs"), None),
        P(("blk", "crs")),
        P(("blk", "crs")),
        P(None, ("blk", "crs")),
        P(None, ("blk", "crs")),
        P(None, ("blk", "crs")),
        P(("blk", "crs")),
        P(("blk", "crs"), None),
    )
    out_specs = (P("blk", "crs", None), P(None, ("blk", "crs")), P(None, ("blk", "crs")))
    return jax.shard_map(on_device, mesh=mesh, in_specs=in_specs, out_specs=out_specs, check_vma=False)
```

```python
import jax
import jax.numpy as jnp
from jax import lax
from jax.experimental import pallas as pl
from jax.experimental.pallas import tpu as pltpu
from jax.sharding import PartitionSpec as P

TX, TY, L, KN, ITERS = 16, 8, 128, 6, 3
HALO = ITERS
EX = TX + 2 * HALO
EY = 16
TILES = EX * EY
PLANES = 7
K = 32
CAP = 64
F32, BF16, I32 = jnp.float32, jnp.bfloat16, jnp.int32
NT = (((1,), (1,)), ((), ()))
NN = (((1,), (0,)), ((), ()))
TN = (((0,), (0,)), ((), ()))


def dot(a, b, dims):
    return lax.dot_general(a, b, dims, preferred_element_type=F32)


def split3(x):
    high = x.astype(BF16).astype(F32)
    rest = x - high
    mid = rest.astype(BF16).astype(F32)
    return high, mid, rest - mid


def iota(shape, dim):
    return lax.broadcasted_iota(I32, shape, dim)


def distance_rows(xyz):
    left, right = [], []
    for comp in xyz:
        h, m, l = split3(comp)
        left += [2 * h, 2 * m, 2 * h, 2 * l, 2 * h, 2 * m]
        right += [h, h, m, h, l, m]
    norm = xyz[0] * xyz[0] + xyz[1] * xyz[1] + xyz[2] * xyz[2]
    one = jnp.ones_like(norm)
    left += list(split3(1.0 - norm)) + [one] * 3
    right += [one] * 3 + list(split3(-norm))
    return left, right


def store_rows(stage, rows, first, count):
    for k, row in enumerate(rows):
        stage[pl.ds(first * K + k, count, stride=K), :] = row


def cube(t):
    w = jnp.maximum(t, 0.0)
    return w * w * w


def column_sum(acc):
    return jnp.sum(acc.T, axis=0, keepdims=True)


def prep_kernel(contact_ref, owner_ref, pos_ref, vel_ref, mass_ref, rank_ref, base_ref, gain_ref, stage_a, stage_b):
    owner = owner_ref[...]
    upper = (iota((256, 256), 0) < iota((256, 256), 1)).astype(BF16)
    every = jnp.ones((256, 256), BF16)
    carry = jnp.zeros((64, 256), F32)
    for q in range(0, owner.shape[1], 256):
        named = iota((64, 256), 0) == owner[:, q : q + 256]
        hot = named.astype(F32).astype(BF16)
        before = dot(hot, upper, NN) + carry
        rank_ref[:, q : q + 256] = jnp.sum(jnp.where(named, before, 0.0), axis=0, keepdims=True).astype(I32)
        carry = carry + dot(hot, every, NN)
    tiles = vel_ref.shape[1]
    stage_a[...] = jnp.zeros_like(stage_a)
    stage_b[...] = jnp.zeros_like(stage_b)
    left, right = distance_rows([pos_ref[c] for c in range(3)])
    store_rows(stage_a, left, 0, tiles)
    store_rows(stage_b, right, 0, tiles)
    gain = 0.1 / mass_ref[...]
    gain_ref[...] = gain
    for t in range(tiles):
        a = stage_a[t * K : (t + 1) * K, :].astype(BF16)
        total = jnp.zeros((L, L), F32)
        applied = [jnp.zeros((L, L), F32) for _ in range(3)]
        for k in range(4):
            n = contact_ref[t * 4 + k]
            b = stage_b[pl.ds(pl.multiple_of(n * K, K), K), :].astype(BF16)
            w = cube(dot(a, b, TN))
            total = total + w
            for c in range(3):
                applied[c] = applied[c] + w * vel_ref[c, pl.ds(n, 1), :]
        total = column_sum(total)
        for c in range(3):
            own = vel_ref[c, t : t + 1, :]
            contact = (column_sum(applied[c]) - total * own) * (4.0 / 512)
            base_ref[c, t : t + 1, :] = own + gain[t : t + 1, :] * contact


def fluid_kernel(
    own_pos, own_press, own_src, own_res, own_dir, ylow, yhigh, xlow, xhigh, owner_ref, rank_ref, fluid_ref, grain_ref, normal_ref,
    press_ref, send_ref,
    ext, near_v, near_s, stage, left_s, right_s, num_s, deg_s, kept, sem,
):
    blk, crs = lax.axis_index("blk"), lax.axis_index("crs")
    blks, crss = lax.axis_size("blk"), lax.axis_size("crs")
    ext[:, HALO * EY : (HALO + TX) * EY, :] = jnp.zeros((PLANES, TX * EY, L), F32)
    for x in range(HALO):
        for p in range(PLANES):
            ext[p, x * EY : (x + 1) * EY, :] = xlow[p, x]
            ext[p, (HALO + TX + x) * EY : (HALO + TX + x + 1) * EY, :] = xhigh[p, x]
    for x in range(TX):
        r = (HALO + x) * EY
        for p, plane in enumerate((own_pos.at[0], own_pos.at[1], own_pos.at[2], own_press, own_src, own_res, own_dir)):
            ext[p, r : r + TY, :] = plane[x]
            ext[p, r + TY : r + TY + HALO, :] = yhigh[p, x]
            ext[p, r + EY - HALO : r + EY, :] = ylow[p, x]
    stage[...] = jnp.zeros_like(stage)

    def find(ex, _):
        r = pl.multiple_of(ex * EY, EY)
        way = ext[6, pl.ds(r, EY), :].astype(I32)
        dx = lax.shift_right_logical(way * 11, 5)
        dy = way - 3 * dx - 1
        near_v[pl.ds(r, EY), :] = (ex + dx - 1) * EY + ((iota((EY, L), 0) + dy) & (EY - 1))
        return 0

    lax.fori_loop(0, EX, find, 0)
    copy = pltpu.make_async_copy(near_v, near_s, sem)
    copy.start()

    def build(ex, _):
        r = pl.multiple_of(ex * EY, EY)
        left, right = distance_rows([ext[c, pl.ds(r, EY), :] for c in range(3)])
        for rows, target in ((left, left_s), (right, right_s)):
            for half in range(0, EY, 8):
                store_rows(stage, [row[half : half + 8] for row in rows], half, 8)
            target[pl.ds(pl.multiple_of(r * K, EY * K), EY * K), :] = stage[...].astype(BF16)
        return 0

    lax.fori_loop(0, EX, build, 0)
    copy.wait()

    def one_tile(t, with_deg, slot=None):
        a = left_s[pl.ds(pl.multiple_of(t * K, K), K), :]
        acc = jnp.zeros((L, L), F32)
        tot = jnp.zeros((L, L), F32)
        for k in range(0, KN, 2):
            n = [near_s[t, k + e] for e in range(2)]
            b = jnp.concatenate([right_s[pl.ds(pl.multiple_of(m * K, K), K), :] for m in n], axis=1)
            w = cube(dot(a, b, TN))
            for e in range(2):
                part = w[:, e * L : (e + 1) * L]
                if slot is not None:
                    kept[slot, k + e] = part
                acc = acc + part * ext[3, pl.ds(n[e], 1), :]
                if with_deg:
                    tot = tot + part
        num_s[pl.ds(t, 1), :] = column_sum(acc)
        if with_deg:
            deg_s[pl.ds(t, 1), :] = column_sum(tot)

    def kept_tile(t, slot):
        acc = jnp.zeros((L, L), F32)
        for k in range(KN):
            acc = acc + kept[slot, k] * ext[3, pl.ds(near_s[t, k], 1), :]
        num_s[pl.ds(t, 1), :] = column_sum(acc)

    for step in range(ITERS):
        ring = ITERS - 1 - step

        def outer_row(i, _):
            x = HALO - ring + i + jnp.where(i >= ring, TX, 0)
            for y in range(-ring, TY + ring):
                one_tile(x * EY + y % EY, step == 0)
            return 0

        def own_row(i, _):
            for y in range(-ring, TY + ring):
                t = (i + HALO) * EY + y % EY
                if y < 0 or y >= TY:
                    one_tile(t, step == 0)
                elif step == 0:
                    one_tile(t, True, i * TY + y)
                else:
                    kept_tile(t, i * TY + y)
            return 0

        def own_rows(i, _):
            own_row(2 * i, 0)
            return own_row(2 * i + 1, 0)

        if ring:
            lax.fori_loop(0, 2 * ring, outer_row, 0)
            lax.fori_loop(0, TX, own_row, 0)
        else:
            lax.fori_loop(0, TX // 2, own_rows, 0)

        def divide(x, _):
            r = pl.multiple_of(x * EY, EY)
            rows = pl.ds(r, EY)
            y = iota((EY, L), 0)
            y = jnp.where(y >= EY - HALO, y - EY, y)
            gy = y + crs * TY
            gx = x - HALO + blk * TX
            inside = (gy >= 0) & (gy < crss * TY) & (gx >= 0) & (gx < blks * TX)
            scale = 1.0 / (KN * L)
            new = (ext[4, rows, :] + num_s[rows, :] * scale) / (deg_s[rows, :] * scale + ext[5, rows, :])
            ext[3, rows, :] = jnp.where(inside, new, 0.0)
            return 0

        lax.fori_loop(HALO - ring, HALO + TX + ring, divide, 0)
    for x in range(TX):
        press_ref[x] = ext[3, (HALO + x) * EY : (HALO + x) * EY + TY, :]
    press = press_ref[...].reshape(TX * TY, L)
    parts = jnp.concatenate([s.astype(BF16) for s in split3(press)], axis=1)
    total01 = jnp.zeros((64, L), F32)
    total23 = jnp.zeros((64, L), F32)
    chunk = 512
    for q in range(0, owner_ref.shape[1], chunk):
        cols = slice(q, q + chunk)
        fluid = fluid_ref[:, cols]
        lane = (iota((L, chunk), 0) == (fluid & (L - 1))).astype(F32).astype(BF16)
        found = dot(parts, jnp.concatenate([lane] * 3, axis=0), NN)
        tile = iota((TX * TY, chunk), 0) == lax.shift_right_logical(fluid, 7)
        at = jnp.sum(jnp.where(tile, found, 0.0), axis=0, keepdims=True)
        owned = iota((64, chunk), 0) == owner_ref[:, cols]
        slot = iota((L, chunk), 0)
        rank = rank_ref[:, cols]
        low = (slot == rank).astype(F32).astype(BF16)
        high = (slot == rank + CAP).astype(F32).astype(BF16)
        rows = [at * normal_ref[c : c + 1, cols] for c in range(3)] + [grain_ref[:, cols].astype(F32)]

        def spread(first, second, hot):
            parts = split3(first) + split3(second)
            out = dot(jnp.concatenate([jnp.where(owned, part, 0.0).astype(BF16) for part in parts], axis=0), hot, NT)
            out = [out[i * 64 : (i + 1) * 64] for i in range(6)]
            return out[0] + out[1] + out[2], out[3] + out[4] + out[5]

        low0, low2 = spread(rows[0], rows[2], low)
        high1, high3 = spread(rows[1], rows[3], high)
        total01 = total01 + low0 + high1
        total23 = total23 + low2 + high3
    send_ref[:, 0, :] = total01
    send_ref[:, 1, :] = total23


def grain_kernel(got_ref, base_ref, gain_ref, new_ref, back_ref):
    count = got_ref.shape[1]
    grain = got_ref[3:4, :].astype(I32)
    tile = iota((8, count), 0) == lax.shift_right_logical(grain, 7)
    lane = (iota((L, count), 0) == (grain & (L - 1))).astype(F32).astype(BF16)
    rows = []
    for c in range(3):
        for part in split3(got_ref[c : c + 1, :]):
            rows.append(jnp.where(tile, part, 0.0))
    summed = dot(jnp.concatenate(rows, axis=0).astype(BF16), lane, NT)
    new = []
    for c in range(3):
        coupling = summed[c * 24 : c * 24 + 8] + summed[c * 24 + 8 : c * 24 + 16] + summed[c * 24 + 16 : c * 24 + 24]
        new.append(base_ref[c] + gain_ref[...] * coupling)
        for g in range(8):
            new_ref[c : c + 1, g * L : (g + 1) * L] = new[c][g : g + 1]
    parts = jnp.concatenate([s.astype(BF16) for s in split3(jnp.concatenate(new, axis=0))], axis=1)
    found = dot(parts, jnp.concatenate([lane] * 3, axis=0), NN)
    for c in range(3):
        back_ref[c : c + 1, :] = jnp.sum(jnp.where(tile, found[c * 8 : c * 8 + 8], 0.0), axis=0, keepdims=True)


def pick_kernel(got_ref, owner_ref, rank_ref, out_ref):
    blocks = jnp.concatenate([got_ref[:, c * CAP : (c + 1) * CAP] for c in range(3)], axis=0)
    parts = [s.astype(BF16) for s in split3(blocks)]
    chunk = 512
    for q in range(0, owner_ref.shape[1], chunk):
        cols = slice(q, q + chunk)
        slot = (iota((CAP, chunk), 0) == rank_ref[:, cols]).astype(F32).astype(BF16)
        found = dot(parts[0], slot, NN) + dot(parts[1], slot, NN) + dot(parts[2], slot, NN)
        owned = iota((64, chunk), 0) == owner_ref[:, cols]
        for c in range(3):
            out_ref[c : c + 1, cols] = jnp.sum(jnp.where(owned, found[c * 64 : (c + 1) * 64], 0.0), axis=0, keepdims=True)


VMEM = pl.BlockSpec(memory_space=pltpu.VMEM)
SMEM = pl.BlockSpec(memory_space=pltpu.SMEM)


def shape(*dims, dtype=F32):
    return jax.ShapeDtypeStruct(dims, dtype)


def cost(flops, size):
    return pl.CostEstimate(flops=flops, bytes_accessed=size, transcendentals=0)


def shifts(axis):
    count = lax.axis_size(axis)
    forward = [(i, (i + 1) % count) for i in range(count)]
    return forward, [(b, a) for a, b in forward]


def exchange(axis, up, down):
    forward, backward = shifts(axis)
    here = lax.axis_index(axis)
    up = jnp.where(here == lax.axis_size(axis) - 1, 0.0, up)
    down = jnp.where(here == 0, 0.0, down)
    return lax.ppermute(up, axis, forward), lax.ppermute(down, axis, backward)


def on_device(positions, pressure_start, source, resist, neighbour_tiles, pair_owner, pair_fluid, pair_grain, pair_normal,
              grain_positions, grain_velocity, grain_mass, contact_tiles):
    pairs = pair_fluid.shape[0]
    owner = pair_owner.reshape(1, pairs)
    fluid = pair_fluid.reshape(1, pairs)
    grain = pair_grain.reshape(1, pairs)
    here_x = jnp.arange(TX, dtype=I32)[:, None, None]
    here_y = jnp.arange(TY, dtype=I32)[None, :, None]
    way = (neighbour_tiles // (TY + 2) - here_x) * 3 + neighbour_tiles % (TY + 2) - here_y
    way = jnp.pad(way.astype(F32), ((0, 0), (0, 0), (0, L - KN)))

    def planes(xs, ys):
        return jnp.concatenate(
            [positions[:, xs, ys], pressure_start[None, xs, ys], source[None, xs, ys], resist[None, xs, ys], way[None, xs, ys]], axis=0
        )

    every, first, last = slice(None), slice(0, HALO), slice(-HALO, None)
    ylow, yhigh = exchange("crs", planes(every, last), planes(every, first))
    gap = jnp.zeros((PLANES, HALO, EY - TY - 2 * HALO, L), F32)

    def wide(xs):
        return jnp.concatenate([planes(xs, every), yhigh[:, xs], gap, ylow[:, xs]], axis=2)

    xlow, xhigh = exchange("blk", wide(last), wide(first))

    grain_tiles = grain_mass.shape[0] // L
    rank, base, gain = pl.pallas_call(
        prep_kernel,
        out_shape=(shape(1, pairs, dtype=I32), shape(3, grain_tiles, L), shape(grain_tiles, L)),
        in_specs=[SMEM] + [VMEM] * 4,
        out_specs=(VMEM,) * 3,
        scratch_shapes=[pltpu.VMEM((grain_tiles * K, L), F32)] * 2,
        compiler_params=pltpu.CompilerParams(vmem_limit_bytes=32 << 20),
        cost_estimate=cost(10**9, 10**6),
        name="prep",
    )(contact_tiles.reshape(-1), owner, grain_positions.reshape(3, grain_tiles, L), grain_velocity.reshape(3, grain_tiles, L), grain_mass.reshape(grain_tiles, L))

    press, send = pl.pallas_call(
        fluid_kernel,
        out_shape=(shape(TX, TY, L), shape(64, 2, L)),
        in_specs=[VMEM] * 14,
        out_specs=(VMEM,) * 2,
        scratch_shapes=[
            pltpu.VMEM((PLANES, TILES, L), F32),
            pltpu.VMEM((TILES, L), I32),
            pltpu.SMEM((TILES, L), I32),
            pltpu.VMEM((EY * K, L), F32),
            pltpu.VMEM((TILES * K, L), BF16),
            pltpu.VMEM((TILES * K, L), BF16),
            pltpu.VMEM((TILES, L), F32),
            pltpu.VMEM((TILES, L), F32),
            pltpu.VMEM((TX * TY, KN, L, L), F32),
            pltpu.SemaphoreType.DMA,
        ],
        compiler_params=pltpu.CompilerParams(vmem_limit_bytes=60 << 20),
        cost_estimate=cost(10**10, 10**7),
        name="fluid",
    )(positions, pressure_start, source, resist, way, ylow, yhigh, xlow, xhigh, owner, rank, fluid, grain, pair_normal)

    got = lax.all_to_all(send, "blk", 0, 0, tiled=True)
    got = got.reshape(64, 4, CAP).swapaxes(0, 1).reshape(4, 64 * CAP)
    grain_new, back = pl.pallas_call(
        grain_kernel,
        out_shape=(shape(3, grain_tiles * L), shape(3, 64 * CAP)),
        in_specs=[VMEM] * 3,
        out_specs=(VMEM,) * 2,
        compiler_params=pltpu.CompilerParams(vmem_limit_bytes=32 << 20),
        cost_estimate=cost(10**9, 10**6),
        name="grain",
    )(got, base, gain)
    back = back.reshape(3, 64, CAP).swapaxes(0, 1).reshape(64, 3 * CAP)
    seen = lax.all_to_all(back, "blk", 0, 0, tiled=True)
    seen = pl.pallas_call(
        pick_kernel,
        out_shape=shape(3, pairs),
        in_specs=[VMEM] * 3,
        out_specs=VMEM,
        compiler_params=pltpu.CompilerParams(vmem_limit_bytes=32 << 20),
        cost_estimate=cost(10**9, 10**6),
        name="pick",
    )(seen, owner, rank)
    return press, grain_new, seen


def solution(mesh):
    in_specs = (
        P(None, "blk", "crs", None),
        P("blk", "crs", None),
        P("blk", "crs", None),
        P("blk", "crs", None),
        P("blk", "crs", None),
        P(("blk", "crs"), None),
        P(("blk", "crs")),
        P(("blk", "crs")),
        P(None, ("blk", "crs")),
        P(None, ("blk", "crs")),
        P(None, ("blk", "crs")),
        P(("blk", "crs")),
        P(("blk", "crs"), None),
    )
    out_specs = (P("blk", "crs", None), P(None, ("blk", "crs")), P(None, ("blk", "crs")))
    return jax.shard_map(on_device, mesh=mesh, in_specs=in_specs, out_specs=out_specs, check_vma=False)
```

```python
import jax
import jax.numpy as jnp
from jax import lax
from jax.experimental import pallas as pl
from jax.experimental.pallas import tpu as pltpu
from jax.sharding import PartitionSpec as P

TX, TY, L, KN, ITERS = 16, 8, 128, 6, 3
HALO = ITERS
EX = TX + 2 * HALO
EY = 16
TILES = EX * EY
PLANES = 7
K = 32
CAP = 64
F32, BF16, I32 = jnp.float32, jnp.bfloat16, jnp.int32
NT = (((1,), (1,)), ((), ()))
NN = (((1,), (0,)), ((), ()))
TN = (((0,), (0,)), ((), ()))


def dot(a, b, dims):
    return lax.dot_general(a, b, dims, preferred_element_type=F32)


def split3(x):
    high = x.astype(BF16).astype(F32)
    rest = x - high
    mid = rest.astype(BF16).astype(F32)
    return high, mid, rest - mid


def iota(shape, dim):
    return lax.broadcasted_iota(I32, shape, dim)


def distance_rows(xyz):
    left, right = [], []
    for comp in xyz:
        h, m, l = split3(comp)
        left += [2 * h, 2 * m, 2 * h, 2 * l, 2 * h, 2 * m]
        right += [h, h, m, h, l, m]
    norm = xyz[0] * xyz[0] + xyz[1] * xyz[1] + xyz[2] * xyz[2]
    one = jnp.ones_like(norm)
    left += list(split3(1.0 - norm)) + [one] * 3
    right += [one] * 3 + list(split3(-norm))
    return left, right


OWN = slice(HALO, HALO + TX)


def pack_kernel(pos_hbm, press_hbm, src_hbm, res_hbm, near_ref, up_ref, down_ref, way_ref, pos, rest, named_v, sems):
    gets = [
        pltpu.make_async_copy(pos_hbm, pos, sems.at[0]),
        pltpu.make_async_copy(press_hbm, rest.at[0], sems.at[1]),
        pltpu.make_async_copy(src_hbm, rest.at[1], sems.at[2]),
        pltpu.make_async_copy(res_hbm, rest.at[2], sems.at[3]),
    ]
    for get in gets:
        get.start()
    named_v[...] = jnp.zeros_like(named_v)
    named_v[:, :, :TX] = near_ref[...]
    ways = []
    for k in range(KN):
        named = named_v[k]
        ext_x = lax.shift_right_logical(named * 205, 11)
        ways.append((ext_x - iota((TY, L), 1)) * 3 + named - (TY + 2) * ext_x - iota((TY, L), 0))
    lane = iota((TY, L), 1)
    for x in range(TX):
        row = jnp.zeros((TY, L), I32)
        for k in range(KN):
            row = jnp.where(lane == k, pltpu.roll(ways[k], (k - x) % L, 1), row)
        way_ref[x] = row.astype(F32)
    top = lax.axis_index("crs") == lax.axis_size("crs") - 1
    bottom = lax.axis_index("crs") == 0
    for get in gets:
        get.wait()
    for p in range(PLANES):
        plane = pos.at[p] if p < 3 else way_ref if p == 6 else rest.at[p - 3]
        up_ref[p] = jnp.where(top, 0.0, plane[:, TY - HALO :, :])
        down_ref[p] = jnp.where(bottom, 0.0, plane[:, :HALO, :])


def build_half(xyz, stage):
    left, right = distance_rows(xyz)
    for k, row in enumerate(left + right):
        stage[pl.ds(k if k < len(left) else k - len(left) + K, 8, stride=2 * K), :] = row
    return stage[...].astype(BF16).reshape(8, 2 * K, L)


def store_rows(stage, rows, first, count):
    for k, row in enumerate(rows):
        stage[pl.ds(first * K + k, count, stride=K), :] = row


def cube(t):
    w = jnp.maximum(t, 0.0)
    return w * w * w


def column_sum(acc):
    return jnp.sum(acc.T, axis=0, keepdims=True)


def side_kernel(yhigh, ylow, out_ref, ext, stage, lr, sems):
    stage[...] = jnp.zeros_like(stage)
    ext[...] = jnp.zeros_like(ext)
    for c in range(3):
        for x in range(TX):
            ext[c, x, :HALO, :] = yhigh[c, x]
            ext[c, x, 8 - HALO :, :] = ylow[c, x]
    quarter = TX // 4

    def send(i):
        rows = pl.ds(i * quarter, quarter)
        return pltpu.make_async_copy(lr.at[rows], out_ref.at[rows], sems.at[i])

    def build(i, _):
        for e in range(quarter):
            x = i * quarter + e
            lr[x] = build_half([ext[c, x] for c in range(3)], stage)
        send(i).start()
        return 0

    lax.fori_loop(0, 4, build, 0)
    for i in range(4):
        send(i).wait()


def prep_kernel(
    contact_ref, owner_ref, pos_ref, vel_ref, mass_ref, own_pos, own_press, own_src, own_res, own_way,
    rank_ref, base_ref, gain_ref, lr_ref, last_ref, first_ref,
    stage_a, stage_b, vel, stage, lr, sem,
):
    for p, plane in enumerate((own_pos.at[0], own_pos.at[1], own_pos.at[2], own_press, own_src, own_res, own_way)):
        last_ref[p] = plane[TX - HALO :]
        first_ref[p] = plane[:HALO]
    stage[...] = jnp.zeros_like(stage)

    def build(i, _):
        for e in range(4):
            x = i * 4 + e
            lr[x] = build_half([own_pos[c, x] for c in range(3)], stage)
        return 0

    lax.fori_loop(0, TX // 4, build, 0)
    send = pltpu.make_async_copy(lr, lr_ref, sem)
    send.start()
    owner = owner_ref[...]
    upper = (iota((256, 256), 0) < iota((256, 256), 1)).astype(BF16)
    every = jnp.ones((256, 256), BF16)
    carry = jnp.zeros((64, 256), F32)
    for q in range(0, owner.shape[1], 256):
        named = iota((64, 256), 0) == owner[:, q : q + 256]
        hot = named.astype(F32).astype(BF16)
        before = dot(hot, upper, NN) + carry
        rank_ref[:, q : q + 256] = jnp.sum(jnp.where(named, before, 0.0), axis=0, keepdims=True).astype(I32)
        carry = carry + dot(hot, every, NN)
    tiles = mass_ref.shape[0]
    stage_a[...] = jnp.zeros_like(stage_a)
    stage_b[...] = jnp.zeros_like(stage_b)
    def tiled(ref, c):
        return jnp.concatenate([ref[c : c + 1, t * L : (t + 1) * L] for t in range(tiles)], axis=0)

    for c in range(3):
        vel[c] = tiled(vel_ref, c)
    left, right = distance_rows([tiled(pos_ref, c) for c in range(3)])
    store_rows(stage_a, left, 0, tiles)
    store_rows(stage_b, right, 0, tiles)
    gain = 0.1 / mass_ref[...]
    gain_ref[...] = gain
    for t in range(tiles):
        a = stage_a[t * K : (t + 1) * K, :].astype(BF16)
        total = jnp.zeros((L, L), F32)
        applied = [jnp.zeros((L, L), F32) for _ in range(3)]
        for k in range(4):
            n = contact_ref[k, t]
            b = stage_b[pl.ds(pl.multiple_of(n * K, K), K), :].astype(BF16)
            w = cube(dot(a, b, TN))
            total = total + w
            for c in range(3):
                applied[c] = applied[c] + w * vel[c, pl.ds(n, 1), :]
        total = column_sum(total)
        for c in range(3):
            own = vel[c, t : t + 1, :]
            contact = (column_sum(applied[c]) - total * own) * (4.0 / 512)
            base_ref[c, t : t + 1, :] = own + gain[t : t + 1, :] * contact
    send.wait()


def fluid_kernel(
    own_press, own_src, own_res, own_way, ylow, yhigh, xlow, xhigh, lr_own, lr_side, owner_ref, rank_ref, fluid_ref, grain_ref, normal_ref,
    press_ref, send_ref,
    ext, near_v, near_s, stage, lr, num_s, deg_s, kept, sem, in_sem,
):
    blk, crs = lax.axis_index("blk"), lax.axis_index("crs")
    blks, crss = lax.axis_size("blk"), lax.axis_size("crs")
    gets = [
        pltpu.make_async_copy(lr_own, lr.at[OWN, :TY], in_sem.at[0]),
        pltpu.make_async_copy(lr_side, lr.at[OWN, TY:], in_sem.at[1]),
    ]
    for get in gets:
        get.start()
    own = (own_press, own_src, own_res, own_way)
    ext[3:, HALO * EY : (HALO + TX) * EY, :] = jnp.zeros((len(own), TX * EY, L), F32)
    for x in range(HALO):
        for p in range(PLANES):
            ext[p, x * EY : (x + 1) * EY, :] = xlow[p, x]
            ext[p, (HALO + TX + x) * EY : (HALO + TX + x + 1) * EY, :] = xhigh[p, x]
    for x in range(TX):
        r = (HALO + x) * EY
        for p, plane in enumerate(own, 3):
            ext[p, r : r + TY, :] = plane[x]
            ext[p, r + TY : r + TY + HALO, :] = yhigh[p, x]
            ext[p, r + EY - HALO : r + EY, :] = ylow[p, x]
    stage[...] = jnp.zeros_like(stage)

    def find(ex, _):
        r = pl.multiple_of(ex * EY, EY)
        way = ext[6, pl.ds(r, EY), :].astype(I32)
        dx = lax.shift_right_logical(way * 11, 5)
        dy = way - 3 * dx - 1
        near_v[pl.ds(r, EY), :] = (ex + dx - 1) * EY + ((iota((EY, L), 0) + dy) & (EY - 1))
        return 0

    lax.fori_loop(0, EX, find, 0)
    copy = pltpu.make_async_copy(near_v, near_s, sem)
    copy.start()

    def build(i, _):
        ex = i + jnp.where(i >= HALO, TX, 0)
        for half in (0, 8):
            r = pl.multiple_of(ex * EY + half, 8)
            lr[ex, half : half + 8] = build_half([ext[c, pl.ds(r, 8), :] for c in range(3)], stage)
        return 0

    lax.fori_loop(0, 2 * HALO, build, 0)
    for get in gets:
        get.wait()
    copy.wait()

    def one_tile(t, with_deg, slot=None):
        a = lr[lax.shift_right_logical(t, 4), t & (EY - 1), :K, :]
        acc = jnp.zeros((L, L), F32)
        tot = jnp.zeros((L, L), F32)
        for k in range(0, KN, 2):
            n = [near_s[t, k + e] for e in range(2)]
            b = jnp.concatenate([lr[lax.shift_right_logical(m, 4), m & (EY - 1), K:, :] for m in n], axis=1)
            w = cube(dot(a, b, TN))
            for e in range(2):
                part = w[:, e * L : (e + 1) * L]
                if slot is not None:
                    kept[slot, k + e] = part
                acc = acc + part * ext[3, pl.ds(n[e], 1), :]
                if with_deg:
                    tot = tot + part
        num_s[pl.ds(t, 1), :] = column_sum(acc)
        if with_deg:
            deg_s[pl.ds(t, 1), :] = column_sum(tot)

    def kept_tile(t, slot):
        acc = jnp.zeros((L, L), F32)
        for k in range(KN):
            acc = acc + kept[slot, k] * ext[3, pl.ds(near_s[t, k], 1), :]
        num_s[pl.ds(t, 1), :] = column_sum(acc)

    for step in range(ITERS):
        ring = ITERS - 1 - step

        def outer_row(i, _):
            x = HALO - ring + i + jnp.where(i >= ring, TX, 0)
            for y in range(-ring, TY + ring):
                one_tile(x * EY + y % EY, step == 0)
            return 0

        def own_row(i, _):
            for y in range(-ring, TY + ring):
                t = (i + HALO) * EY + y % EY
                if y < 0 or y >= TY:
                    one_tile(t, step == 0)
                elif step == 0:
                    one_tile(t, True, i * TY + y)
                else:
                    kept_tile(t, i * TY + y)
            return 0

        def own_rows(i, _):
            own_row(2 * i, 0)
            return own_row(2 * i + 1, 0)

        if ring:
            lax.fori_loop(0, 2 * ring, outer_row, 0)
            lax.fori_loop(0, TX, own_row, 0)
        else:
            lax.fori_loop(0, TX // 2, own_rows, 0)

        def divide(x, _):
            r = pl.multiple_of(x * EY, EY)
            rows = pl.ds(r, EY)
            y = iota((EY, L), 0)
            y = jnp.where(y >= EY - HALO, y - EY, y)
            gy = y + crs * TY
            gx = x - HALO + blk * TX
            inside = (gy >= 0) & (gy < crss * TY) & (gx >= 0) & (gx < blks * TX)
            scale = 1.0 / (KN * L)
            new = (ext[4, rows, :] + num_s[rows, :] * scale) / (deg_s[rows, :] * scale + ext[5, rows, :])
            ext[3, rows, :] = jnp.where(inside, new, 0.0)
            return 0

        lax.fori_loop(HALO - ring, HALO + TX + ring, divide, 0)
    for x in range(TX):
        press_ref[x] = ext[3, (HALO + x) * EY : (HALO + x) * EY + TY, :]
    press = press_ref[...].reshape(TX * TY, L)
    parts = jnp.concatenate([s.astype(BF16) for s in split3(press)], axis=1)
    total01 = jnp.zeros((64, L), F32)
    total23 = jnp.zeros((64, L), F32)
    chunk = 512
    for q in range(0, owner_ref.shape[1], chunk):
        cols = slice(q, q + chunk)
        fluid = fluid_ref[:, cols]
        lane = (iota((L, chunk), 0) == (fluid & (L - 1))).astype(F32).astype(BF16)
        found = dot(parts, jnp.concatenate([lane] * 3, axis=0), NN)
        tile = iota((TX * TY, chunk), 0) == lax.shift_right_logical(fluid, 7)
        at = jnp.sum(jnp.where(tile, found, 0.0), axis=0, keepdims=True)
        owned = iota((64, chunk), 0) == owner_ref[:, cols]
        slot = iota((L, chunk), 0)
        rank = rank_ref[:, cols]
        low = (slot == rank).astype(F32).astype(BF16)
        high = (slot == rank + CAP).astype(F32).astype(BF16)
        rows = [at * normal_ref[c : c + 1, cols] for c in range(3)] + [grain_ref[:, cols].astype(F32)]

        def spread(first, second, hot):
            parts = split3(first) + split3(second)
            out = dot(jnp.concatenate([jnp.where(owned, part, 0.0).astype(BF16) for part in parts], axis=0), hot, NT)
            out = [out[i * 64 : (i + 1) * 64] for i in range(6)]
            return out[0] + out[1] + out[2], out[3] + out[4] + out[5]

        low0, low2 = spread(rows[0], rows[2], low)
        high1, high3 = spread(rows[1], rows[3], high)
        total01 = total01 + low0 + high1
        total23 = total23 + low2 + high3
    send_ref[:, 0, :] = total01
    send_ref[:, 1, :] = total23


def grain_kernel(got_ref, base_ref, gain_ref, new_ref, back_ref):
    count = got_ref.shape[1]
    grain = got_ref[3:4, :].astype(I32)
    tile = iota((8, count), 0) == lax.shift_right_logical(grain, 7)
    lane = (iota((L, count), 0) == (grain & (L - 1))).astype(F32).astype(BF16)
    rows = []
    for c in range(3):
        for part in split3(got_ref[c : c + 1, :]):
            rows.append(jnp.where(tile, part, 0.0))
    summed = dot(jnp.concatenate(rows, axis=0).astype(BF16), lane, NT)
    new = []
    for c in range(3):
        coupling = summed[c * 24 : c * 24 + 8] + summed[c * 24 + 8 : c * 24 + 16] + summed[c * 24 + 16 : c * 24 + 24]
        new.append(base_ref[c] + gain_ref[...] * coupling)
        for g in range(8):
            new_ref[c : c + 1, g * L : (g + 1) * L] = new[c][g : g + 1]
    parts = jnp.concatenate([s.astype(BF16) for s in split3(jnp.concatenate(new, axis=0))], axis=1)
    found = dot(parts, jnp.concatenate([lane] * 3, axis=0), NN)
    for c in range(3):
        back_ref[c : c + 1, :] = jnp.sum(jnp.where(tile, found[c * 8 : c * 8 + 8], 0.0), axis=0, keepdims=True)


def pick_kernel(got_ref, owner_ref, rank_ref, out_ref):
    blocks = jnp.concatenate([got_ref[:, c * CAP : (c + 1) * CAP] for c in range(3)], axis=0)
    parts = [s.astype(BF16) for s in split3(blocks)]
    chunk = 512
    for q in range(0, owner_ref.shape[1], chunk):
        cols = slice(q, q + chunk)
        slot = (iota((CAP, chunk), 0) == rank_ref[:, cols]).astype(F32).astype(BF16)
        found = dot(parts[0], slot, NN) + dot(parts[1], slot, NN) + dot(parts[2], slot, NN)
        owned = iota((64, chunk), 0) == owner_ref[:, cols]
        for c in range(3):
            out_ref[c : c + 1, cols] = jnp.sum(jnp.where(owned, found[c * 64 : (c + 1) * 64], 0.0), axis=0, keepdims=True)


VMEM = pl.BlockSpec(memory_space=pltpu.VMEM)
SMEM = pl.BlockSpec(memory_space=pltpu.SMEM)
HBM = pl.BlockSpec(memory_space=pltpu.HBM)


def shape(*dims, dtype=F32):
    return jax.ShapeDtypeStruct(dims, dtype)


def cost(flops, size):
    return pl.CostEstimate(flops=flops, bytes_accessed=size, transcendentals=0)


def shifts(axis):
    count = lax.axis_size(axis)
    forward = [(i, (i + 1) % count) for i in range(count)]
    return forward, [(b, a) for a, b in forward]


def on_device(positions, pressure_start, source, resist, neighbour_tiles, pair_owner, pair_fluid, pair_grain, pair_normal,
              grain_positions, grain_velocity, grain_mass, contact_tiles):
    pairs = pair_fluid.shape[0]
    owner = pair_owner.reshape(1, pairs)
    fluid = pair_fluid.reshape(1, pairs)
    grain = pair_grain.reshape(1, pairs)
    semaphore = pltpu.SemaphoreType.DMA
    params = pltpu.CompilerParams(vmem_limit_bytes=62 << 20)
    rim_y, rim_x = shape(PLANES, TX, HALO, L), shape(PLANES, HALO, TY, L)
    up, down, way = pl.pallas_call(
        pack_kernel,
        out_shape=(rim_y, rim_y, shape(TX, TY, L)),
        in_specs=[HBM] * 4 + [VMEM],
        out_specs=(VMEM,) * 3,
        scratch_shapes=[pltpu.VMEM((3, TX, TY, L), F32), pltpu.VMEM((3, TX, TY, L), F32), pltpu.VMEM((KN, TY, L), I32), semaphore((4,))],
        compiler_params=params,
        cost_estimate=cost(10**6, 10**6),
        name="pack",
    )(positions, pressure_start, source, resist, neighbour_tiles.transpose(2, 1, 0))
    forward, backward = shifts("crs")
    ylow = lax.ppermute(up, "crs", forward)
    yhigh = lax.ppermute(down, "crs", backward)
    grain_tiles = grain_mass.shape[0] // L
    half = shape(TX, 8, 2 * K, L, dtype=BF16)
    half_scratch = [pltpu.VMEM((8 * 2 * K, L), F32), pltpu.VMEM((TX, 8, 2 * K, L), BF16)]
    rank, base, gain, lr_own, last, first = pl.pallas_call(
        prep_kernel,
        out_shape=(shape(1, pairs, dtype=I32), shape(3, grain_tiles, L), shape(grain_tiles, L), half, rim_x, rim_x),
        in_specs=[SMEM] + [VMEM] * 9,
        out_specs=(VMEM, VMEM, VMEM, HBM, VMEM, VMEM),
        scratch_shapes=[pltpu.VMEM((grain_tiles * K, L), F32)] * 2 + [pltpu.VMEM((3, grain_tiles, L), F32)] + half_scratch + [semaphore],
        compiler_params=params,
        cost_estimate=cost(10**9, 10**6),
        name="prep",
    )(contact_tiles.T, owner, grain_positions, grain_velocity, grain_mass.reshape(grain_tiles, L), positions, pressure_start, source, resist, way)
    gap = jnp.zeros((PLANES, HALO, EY - TY - 2 * HALO, L), F32)

    def wide(middle, xs):
        return jnp.concatenate([middle, yhigh[:, xs], gap, ylow[:, xs]], axis=2)

    forward, backward = shifts("blk")
    here, count = lax.axis_index("blk"), lax.axis_size("blk")
    xlow = lax.ppermute(jnp.where(here == count - 1, 0.0, wide(last, slice(-HALO, None))), "blk", forward)
    xhigh = lax.ppermute(jnp.where(here == 0, 0.0, wide(first, slice(0, HALO))), "blk", backward)

    lr_side = pl.pallas_call(
        side_kernel,
        out_shape=half,
        in_specs=[VMEM] * 2,
        out_specs=HBM,
        scratch_shapes=[pltpu.VMEM((3, TX, 8, L), F32), *half_scratch, semaphore((4,))],
        compiler_params=params,
        cost_estimate=cost(10**9, 10**6),
        name="side",
    )(yhigh, ylow)

    press, send = pl.pallas_call(
        fluid_kernel,
        out_shape=(shape(TX, TY, L), shape(64, 2, L)),
        in_specs=[VMEM] * 8 + [HBM] * 2 + [VMEM] * 5,
        out_specs=(VMEM,) * 2,
        scratch_shapes=[
            pltpu.VMEM((PLANES, TILES, L), F32),
            pltpu.VMEM((TILES, L), I32),
            pltpu.SMEM((TILES, L), I32),
            pltpu.VMEM((8 * 2 * K, L), F32),
            pltpu.VMEM((EX, EY, 2 * K, L), BF16),
            pltpu.VMEM((TILES, L), F32),
            pltpu.VMEM((TILES, L), F32),
            pltpu.VMEM((TX * TY, KN, L, L), F32),
            semaphore,
            semaphore((2,)),
        ],
        compiler_params=pltpu.CompilerParams(vmem_limit_bytes=62 << 20),
        cost_estimate=cost(10**10, 10**7),
        name="fluid",
    )(pressure_start, source, resist, way, ylow, yhigh, xlow, xhigh, lr_own, lr_side, owner, rank, fluid, grain, pair_normal)

    got = lax.all_to_all(send, "blk", 0, 0, tiled=True)
    got = got.reshape(64, 4, CAP).swapaxes(0, 1).reshape(4, 64 * CAP)
    grain_new, back = pl.pallas_call(
        grain_kernel,
        out_shape=(shape(3, grain_tiles * L), shape(3, 64 * CAP)),
        in_specs=[VMEM] * 3,
        out_specs=(VMEM,) * 2,
        compiler_params=pltpu.CompilerParams(vmem_limit_bytes=32 << 20),
        cost_estimate=cost(10**9, 10**6),
        name="grain",
    )(got, base, gain)
    back = back.reshape(3, 64, CAP).swapaxes(0, 1).reshape(64, 3 * CAP)
    seen = lax.all_to_all(back, "blk", 0, 0, tiled=True)
    seen = pl.pallas_call(
        pick_kernel,
        out_shape=shape(3, pairs),
        in_specs=[VMEM] * 3,
        out_specs=VMEM,
        compiler_params=pltpu.CompilerParams(vmem_limit_bytes=32 << 20),
        cost_estimate=cost(10**9, 10**6),
        name="pick",
    )(seen, owner, rank)
    return press, grain_new, seen


def solution(mesh):
    in_specs = (
        P(None, "blk", "crs", None),
        P("blk", "crs", None),
        P("blk", "crs", None),
        P("blk", "crs", None),
        P("blk", "crs", None),
        P(("blk", "crs"), None),
        P(("blk", "crs")),
        P(("blk", "crs")),
        P(None, ("blk", "crs")),
        P(None, ("blk", "crs")),
        P(None, ("blk", "crs")),
        P(("blk", "crs")),
        P(("blk", "crs"), None),
    )
    out_specs = (P("blk", "crs", None), P(None, ("blk", "crs")), P(None, ("blk", "crs")))
    return jax.shard_map(on_device, mesh=mesh, in_specs=in_specs, out_specs=out_specs, check_vma=False)
```

```python
import jax
import jax.numpy as jnp
from jax import lax
from jax.experimental import pallas as pl
from jax.experimental.pallas import tpu as pltpu
from jax.sharding import PartitionSpec as P

TX, TY, L, KN, ITERS = 16, 8, 128, 6, 3
HALO = ITERS
EX = TX + 2 * HALO
EY = 16
TILES = EX * EY
NEAR = -(-TILES // 128) * 128
PLANES = 7
K = 48
CAP = 64
F32, BF16, I32 = jnp.float32, jnp.bfloat16, jnp.int32
NT = (((1,), (1,)), ((), ()))
NN = (((1,), (0,)), ((), ()))
TN = (((0,), (0,)), ((), ()))


def dot(a, b, dims):
    return lax.dot_general(a, b, dims, preferred_element_type=F32)


def split3(x):
    high = x.astype(BF16).astype(F32)
    rest = x - high
    mid = rest.astype(BF16).astype(F32)
    return high, mid, rest - mid


def thirds(x):
    size = x.shape[0] // 3
    return x[:size] + x[size : 2 * size] + x[2 * size :]


def iota(shape, dim):
    return lax.broadcasted_iota(I32, shape, dim)


def pack_kernel(pos_hbm, press_hbm, src_hbm, res_hbm, near_ref, up_ref, down_ref, way_ref, pos, rest, named_v, sems):
    gets = [
        pltpu.make_async_copy(pos_hbm, pos, sems.at[0]),
        pltpu.make_async_copy(press_hbm, rest.at[0], sems.at[1]),
        pltpu.make_async_copy(src_hbm, rest.at[1], sems.at[2]),
        pltpu.make_async_copy(res_hbm, rest.at[2], sems.at[3]),
    ]
    for get in gets:
        get.start()
    named_v[...] = jnp.zeros_like(named_v)
    named_v[:, :, :TX] = near_ref[...]
    ways = []
    for k in range(KN):
        named = named_v[k]
        ext_x = lax.shift_right_logical(named * 205, 11)
        ways.append((ext_x - iota((TY, L), 1)) * 3 + named - (TY + 2) * ext_x - iota((TY, L), 0))
    lane = iota((TY, L), 1)
    for x in range(TX):
        row = jnp.zeros((TY, L), I32)
        for k in range(KN):
            row = jnp.where(lane == k, pltpu.roll(ways[k], (k - x) % L, 1), row)
        way_ref[x] = row.astype(F32)
    top = lax.axis_index("crs") == lax.axis_size("crs") - 1
    bottom = lax.axis_index("crs") == 0
    for get in gets:
        get.wait()
    for p in range(PLANES):
        plane = pos.at[p] if p < 3 else way_ref if p == 6 else rest.at[p - 3]
        up_ref[p] = jnp.where(top, 0.0, plane[:, TY - HALO :, :])
        down_ref[p] = jnp.where(bottom, 0.0, plane[:, :HALO, :])


def clear_stage(stage):
    row = iota((64, L), 0) & 7
    for place, hot in ((0, 3), (1, 4)):
        stage[place] = (row == hot).astype(F32)


def build_half(xyz, stage):
    norm = xyz[0] * xyz[0] + xyz[1] * xyz[1] + xyz[2] * xyz[2]
    left = (2 * xyz[0], 2 * xyz[1], 2 * xyz[2], None, 1.0 - norm)
    right = (xyz[0], xyz[1], xyz[2], -norm)
    for place, rows in enumerate((left, right)):
        for k, row in enumerate(rows):
            if row is not None:
                stage[place, pl.ds(k, 8, stride=8), :] = row
    lh, lm, ll = split3(stage[0].reshape(8, 8, L))
    rh, rm, rl = split3(stage[1].reshape(8, 8, L))
    return jnp.concatenate([lh, lm, lh, ll, lh, lm, rh, rh, rm, rh, rl, rm], axis=1).astype(BF16)


def cube(t):
    w = jnp.maximum(t, 0.0)
    return w * w * w


def column_sum(acc):
    return jnp.sum(acc.T, axis=0, keepdims=True)


def prep_kernel(
    contact_ref, owner_ref, pos_ref, vel_ref, mass_ref, own_pos, own_press, own_src, own_res, own_way,
    rank_ref, base_ref, gain_ref, last_ref, first_ref,
    stage, lr, vel,
):
    for p, plane in enumerate((own_pos.at[0], own_pos.at[1], own_pos.at[2], own_press, own_src, own_res, own_way)):
        last_ref[p] = plane[TX - HALO :]
        first_ref[p] = plane[:HALO]
    owner = owner_ref[...]
    upper = (iota((256, 256), 0) < iota((256, 256), 1)).astype(BF16)
    every = jnp.ones((256, 256), BF16)
    carry = jnp.zeros((64, 256), F32)
    for q in range(0, owner.shape[1], 256):
        named = iota((64, 256), 0) == owner[:, q : q + 256]
        hot = named.astype(F32).astype(BF16)
        before = dot(hot, upper, NN) + carry
        rank_ref[:, q : q + 256] = jnp.sum(jnp.where(named, before, 0.0), axis=0, keepdims=True).astype(I32)
        carry = carry + dot(hot, every, NN)
    tiles = mass_ref.shape[0]
    clear_stage(stage)
    def tiled(ref, c):
        return jnp.concatenate([ref[c : c + 1, t * L : (t + 1) * L] for t in range(tiles)], axis=0)

    for c in range(3):
        vel[c] = tiled(vel_ref, c)
    lr[...] = build_half([tiled(pos_ref, c) for c in range(3)], stage)
    gain = 0.1 / mass_ref[...]
    gain_ref[...] = gain
    for t in range(tiles):
        a = lr[t, :K, :]
        total = jnp.zeros((L, L), F32)
        applied = [jnp.zeros((L, L), F32) for _ in range(3)]
        for k in range(4):
            n = contact_ref[k, t]
            w = cube(dot(a, lr[n, K:, :], TN))
            total = total + w
            for c in range(3):
                applied[c] = applied[c] + w * vel[c, pl.ds(n, 1), :]
        total = column_sum(total)
        for c in range(3):
            own = vel[c, t : t + 1, :]
            contact = (column_sum(applied[c]) - total * own) * (4.0 / 512)
            base_ref[c, t : t + 1, :] = own + gain[t : t + 1, :] * contact


def fluid_kernel(
    own_pos, own_press, own_src, own_res, own_way, ylow, yhigh, xlow, xhigh, owner_ref, rank_ref, fluid_ref, grain_ref, normal_ref,
    press_ref, send_ref,
    ext, near_v, near_t, near_s, stage, lr, num_s, deg_s, kept, sem,
):
    blk, crs = lax.axis_index("blk"), lax.axis_index("crs")
    blks, crss = lax.axis_size("blk"), lax.axis_size("crs")
    own = (own_pos.at[0], own_pos.at[1], own_pos.at[2], own_press, own_src, own_res, own_way)
    ext[:, HALO * EY : (HALO + TX) * EY, :] = jnp.zeros((PLANES, TX * EY, L), F32)

    def fill(planes):
        for p in planes:
            for x in range(HALO):
                ext[p, x * EY : (x + 1) * EY, :] = xlow[p, x]
                ext[p, (HALO + TX + x) * EY : (HALO + TX + x + 1) * EY, :] = xhigh[p, x]
            for x in range(TX):
                r = (HALO + x) * EY
                ext[p, r : r + TY, :] = own[p][x]
                ext[p, r + TY : r + TY + HALO, :] = yhigh[p, x]
                ext[p, r + EY - HALO : r + EY, :] = ylow[p, x]

    fill([6])

    def find(ex, _):
        r = pl.multiple_of(ex * EY, EY)
        way = ext[6, pl.ds(r, EY), :].astype(I32)
        dx = lax.shift_right_logical(way * 11, 5)
        dy = way - 3 * dx - 1
        near_v[pl.ds(r, EY), :] = ((ex + dx - 1) * EY + ((iota((EY, L), 0) + dy) & (EY - 1))).astype(F32)
        return 0

    lax.fori_loop(0, EX, find, 0)
    near_v[TILES:, :] = jnp.zeros((NEAR - TILES, L), F32)
    for t in range(0, NEAR, L):
        near_t[:, t : t + L] = near_v[t : t + L, :].T[:8].astype(I32)
    copy = pltpu.make_async_copy(near_t, near_s, sem)
    copy.start()

    fill(range(6))
    for e in range(4):
        clear_stage(stage.at[e])

    def build(i, _):
        for e in range(4):
            ex = 2 * i + e // 2
            half = e % 2 * 8
            r = pl.multiple_of(ex * EY + half, 8)
            lr[pl.ds(r, 8)] = build_half([ext[c, pl.ds(r, 8), :] for c in range(3)], stage.at[e])
        return 0

    lax.fori_loop(0, EX // 2, build, 0)
    copy.wait()

    def one_tile(t, with_deg, slot=None):
        a = lr[t, :K, :]
        acc = jnp.zeros((L, L), F32)
        tot = jnp.zeros((L, L), F32)
        for k in range(0, KN, 2):
            n = [near_s[k + e, t] for e in range(2)]
            b = jnp.concatenate([lr[m, K:, :] for m in n], axis=1)
            w = cube(dot(a, b, TN))
            for e in range(2):
                part = w[:, e * L : (e + 1) * L]
                if slot is not None:
                    kept[slot, k + e] = part
                acc = acc + part * ext[3, pl.ds(n[e], 1), :]
                if with_deg:
                    tot = tot + part
        num_s[pl.ds(t, 1), :] = column_sum(acc)
        if with_deg:
            deg_s[pl.ds(t, 1), :] = column_sum(tot)

    def kept_tile(t, slot):
        acc = jnp.zeros((L, L), F32)
        for k in range(KN):
            acc = acc + kept[slot, k] * ext[3, pl.ds(near_s[k, t], 1), :]
        num_s[pl.ds(t, 1), :] = column_sum(acc)

    for step in range(ITERS):
        ring = ITERS - 1 - step

        def outer_row(i, _):
            x = HALO - ring + i + jnp.where(i >= ring, TX, 0)
            for y in range(-ring, TY + ring):
                one_tile(x * EY + y % EY, step == 0)
            return 0

        def own_row(i, _):
            for y in range(-ring, TY + ring):
                t = (i + HALO) * EY + y % EY
                if y < 0 or y >= TY:
                    one_tile(t, step == 0)
                elif step == 0:
                    one_tile(t, True, i * TY + y)
                else:
                    kept_tile(t, i * TY + y)
            return 0

        def own_rows(i, _):
            own_row(2 * i, 0)
            return own_row(2 * i + 1, 0)

        if ring:
            lax.fori_loop(0, 2 * ring, outer_row, 0)
            lax.fori_loop(0, TX, own_row, 0)
        else:
            lax.fori_loop(0, TX // 2, own_rows, 0)

        def divide(x, _):
            r = pl.multiple_of(x * EY, EY)
            rows = pl.ds(r, EY)
            y = iota((EY, L), 0)
            y = jnp.where(y >= EY - HALO, y - EY, y)
            gy = y + crs * TY
            gx = x - HALO + blk * TX
            inside = (gy >= 0) & (gy < crss * TY) & (gx >= 0) & (gx < blks * TX)
            scale = 1.0 / (KN * L)
            new = (ext[4, rows, :] + num_s[rows, :] * scale) / (deg_s[rows, :] * scale + ext[5, rows, :])
            ext[3, rows, :] = jnp.where(inside, new, 0.0)
            return 0

        lax.fori_loop(HALO - ring, HALO + TX + ring, divide, 0)
    for x in range(TX):
        press_ref[x] = ext[3, (HALO + x) * EY : (HALO + x) * EY + TY, :]
    press = press_ref[...].reshape(TX * TY, L)
    parts = jnp.concatenate([s.astype(BF16) for s in split3(press)], axis=0)
    total01 = jnp.zeros((64, L), F32)
    total23 = jnp.zeros((64, L), F32)
    chunk = 512
    for q in range(0, owner_ref.shape[1], chunk):
        cols = slice(q, q + chunk)
        fluid = fluid_ref[:, cols]
        lane = (iota((L, chunk), 0) == (fluid & (L - 1))).astype(F32).astype(BF16)
        found = thirds(dot(parts, lane, NN))
        tile = iota((TX * TY, chunk), 0) == lax.shift_right_logical(fluid, 7)
        at = jnp.sum(jnp.where(tile, found, 0.0), axis=0, keepdims=True)
        owned = iota((64, chunk), 0) == owner_ref[:, cols]
        slot = iota((L, chunk), 0)
        rank = rank_ref[:, cols]
        low = (slot == rank).astype(F32).astype(BF16)
        high = (slot == rank + CAP).astype(F32).astype(BF16)
        rows = [at * normal_ref[c : c + 1, cols] for c in range(3)] + [grain_ref[:, cols].astype(F32)]

        def spread(first, second, hot):
            parts = split3(first) + split3(second)
            out = dot(jnp.concatenate([jnp.where(owned, part, 0.0).astype(BF16) for part in parts], axis=0), hot, NT)
            out = [out[i * 64 : (i + 1) * 64] for i in range(6)]
            return out[0] + out[1] + out[2], out[3] + out[4] + out[5]

        low0, low2 = spread(rows[0], rows[2], low)
        high1, high3 = spread(rows[1], rows[3], high)
        total01 = total01 + low0 + high1
        total23 = total23 + low2 + high3
    send_ref[:, 0, :] = total01
    send_ref[:, 1, :] = total23


def grain_kernel(got_ref, base_ref, gain_ref, new_ref, back_ref):
    count = got_ref.shape[1]
    grain = got_ref[3:4, :].astype(I32)
    tile = iota((8, count), 0) == lax.shift_right_logical(grain, 7)
    lane = (iota((L, count), 0) == (grain & (L - 1))).astype(F32).astype(BF16)
    rows = []
    for c in range(3):
        for part in split3(got_ref[c : c + 1, :]):
            rows.append(jnp.where(tile, part, 0.0))
    summed = dot(jnp.concatenate(rows, axis=0).astype(BF16), lane, NT)
    new = []
    for c in range(3):
        coupling = summed[c * 24 : c * 24 + 8] + summed[c * 24 + 8 : c * 24 + 16] + summed[c * 24 + 16 : c * 24 + 24]
        new.append(base_ref[c] + gain_ref[...] * coupling)
        for g in range(8):
            new_ref[c : c + 1, g * L : (g + 1) * L] = new[c][g : g + 1]
    parts = jnp.concatenate([s for s in split3(jnp.concatenate(new, axis=0))], axis=0).astype(BF16)
    found = thirds(dot(parts, lane, NN))
    for c in range(3):
        back_ref[c : c + 1, :] = jnp.sum(jnp.where(tile, found[c * 8 : c * 8 + 8], 0.0), axis=0, keepdims=True)


def pick_kernel(got_ref, owner_ref, rank_ref, out_ref):
    blocks = jnp.concatenate([got_ref[:, c * CAP : (c + 1) * CAP] for c in range(3)], axis=0)
    parts = jnp.concatenate([s.astype(BF16) for s in split3(blocks)], axis=0)
    chunk = 512
    for q in range(0, owner_ref.shape[1], chunk):
        cols = slice(q, q + chunk)
        slot = (iota((CAP, chunk), 0) == rank_ref[:, cols]).astype(F32).astype(BF16)
        found = thirds(dot(parts, slot, NN))
        owned = iota((64, chunk), 0) == owner_ref[:, cols]
        for c in range(3):
            out_ref[c : c + 1, cols] = jnp.sum(jnp.where(owned, found[c * 64 : (c + 1) * 64], 0.0), axis=0, keepdims=True)


VMEM = pl.BlockSpec(memory_space=pltpu.VMEM)
SMEM = pl.BlockSpec(memory_space=pltpu.SMEM)
HBM = pl.BlockSpec(memory_space=pltpu.HBM)


def shape(*dims, dtype=F32):
    return jax.ShapeDtypeStruct(dims, dtype)


def cost(flops, size):
    return pl.CostEstimate(flops=flops, bytes_accessed=size, transcendentals=0)


def shifts(axis):
    count = lax.axis_size(axis)
    forward = [(i, (i + 1) % count) for i in range(count)]
    return forward, [(b, a) for a, b in forward]


def on_device(positions, pressure_start, source, resist, neighbour_tiles, pair_owner, pair_fluid, pair_grain, pair_normal,
              grain_positions, grain_velocity, grain_mass, contact_tiles):
    pairs = pair_fluid.shape[0]
    owner = pair_owner.reshape(1, pairs)
    fluid = pair_fluid.reshape(1, pairs)
    grain = pair_grain.reshape(1, pairs)
    semaphore = pltpu.SemaphoreType.DMA
    params = pltpu.CompilerParams(vmem_limit_bytes=63 << 20)
    rim_y, rim_x = shape(PLANES, TX, HALO, L), shape(PLANES, HALO, TY, L)
    up, down, way = pl.pallas_call(
        pack_kernel,
        out_shape=(rim_y, rim_y, shape(TX, TY, L)),
        in_specs=[HBM] * 4 + [VMEM],
        out_specs=(VMEM,) * 3,
        scratch_shapes=[pltpu.VMEM((3, TX, TY, L), F32), pltpu.VMEM((3, TX, TY, L), F32), pltpu.VMEM((KN, TY, L), I32), semaphore((4,))],
        compiler_params=params,
        cost_estimate=cost(10**6, 10**6),
        name="pack",
    )(positions, pressure_start, source, resist, neighbour_tiles.transpose(2, 1, 0))
    forward, backward = shifts("crs")
    ylow = lax.ppermute(up, "crs", forward)
    yhigh = lax.ppermute(down, "crs", backward)
    grain_tiles = grain_mass.shape[0] // L
    rank, base, gain, last, first = pl.pallas_call(
        prep_kernel,
        out_shape=(shape(1, pairs, dtype=I32), shape(3, grain_tiles, L), shape(grain_tiles, L), rim_x, rim_x),
        in_specs=[SMEM] + [VMEM] * 9,
        out_specs=(VMEM,) * 5,
        scratch_shapes=[pltpu.VMEM((2, 64, L), F32), pltpu.VMEM((grain_tiles, 2 * K, L), BF16)] + [pltpu.VMEM((3, grain_tiles, L), F32)],
        compiler_params=params,
        cost_estimate=cost(10**9, 10**6),
        name="prep",
    )(contact_tiles.T, owner, grain_positions, grain_velocity, grain_mass.reshape(grain_tiles, L), positions, pressure_start, source, resist, way)
    gap = jnp.zeros((PLANES, HALO, EY - TY - 2 * HALO, L), F32)

    def wide(middle, xs):
        return jnp.concatenate([middle, yhigh[:, xs], gap, ylow[:, xs]], axis=2)

    forward, backward = shifts("blk")
    here, count = lax.axis_index("blk"), lax.axis_size("blk")
    xlow = lax.ppermute(jnp.where(here == count - 1, 0.0, wide(last, slice(-HALO, None))), "blk", forward)
    xhigh = lax.ppermute(jnp.where(here == 0, 0.0, wide(first, slice(0, HALO))), "blk", backward)

    press, send = pl.pallas_call(
        fluid_kernel,
        out_shape=(shape(TX, TY, L), shape(64, 2, L)),
        in_specs=[VMEM] * 14,
        out_specs=(VMEM,) * 2,
        scratch_shapes=[
            pltpu.VMEM((PLANES, TILES, L), F32),
            pltpu.VMEM((NEAR, L), F32),
            pltpu.VMEM((8, NEAR), I32),
            pltpu.SMEM((8, NEAR), I32),
            pltpu.VMEM((4, 2, 64, L), F32),
            pltpu.VMEM((TILES, 2 * K, L), BF16),
            pltpu.VMEM((TILES, L), F32),
            pltpu.VMEM((TILES, L), F32),
            pltpu.VMEM((TX * TY, KN, L, L), F32),
            semaphore,
        ],
        compiler_params=pltpu.CompilerParams(vmem_limit_bytes=63 << 20),
        cost_estimate=cost(10**10, 10**7),
        name="fluid",
    )(positions, pressure_start, source, resist, way, ylow, yhigh, xlow, xhigh, owner, rank, fluid, grain, pair_normal)

    got = lax.all_to_all(send, "blk", 0, 0, tiled=True)
    got = got.reshape(64, 4, CAP).swapaxes(0, 1).reshape(4, 64 * CAP)
    grain_new, back = pl.pallas_call(
        grain_kernel,
        out_shape=(shape(3, grain_tiles * L), shape(3, 64 * CAP)),
        in_specs=[VMEM] * 3,
        out_specs=(VMEM,) * 2,
        compiler_params=pltpu.CompilerParams(vmem_limit_bytes=32 << 20),
        cost_estimate=cost(10**9, 10**6),
        name="grain",
    )(got, base, gain)
    back = back.reshape(3, 64, CAP).swapaxes(0, 1).reshape(64, 3 * CAP)
    seen = lax.all_to_all(back, "blk", 0, 0, tiled=True)
    seen = pl.pallas_call(
        pick_kernel,
        out_shape=shape(3, pairs),
        in_specs=[VMEM] * 3,
        out_specs=VMEM,
        compiler_params=pltpu.CompilerParams(vmem_limit_bytes=32 << 20),
        cost_estimate=cost(10**9, 10**6),
        name="pick",
    )(seen, owner, rank)
    return press, grain_new, seen


def solution(mesh):
    in_specs = (
        P(None, "blk", "crs", None),
        P("blk", "crs", None),
        P("blk", "crs", None),
        P("blk", "crs", None),
        P("blk", "crs", None),
        P(("blk", "crs"), None),
        P(("blk", "crs")),
        P(("blk", "crs")),
        P(None, ("blk", "crs")),
        P(None, ("blk", "crs")),
        P(None, ("blk", "crs")),
        P(("blk", "crs")),
        P(("blk", "crs"), None),
    )
    out_specs = (P("blk", "crs", None), P(None, ("blk", "crs")), P(None, ("blk", "crs")))
    return jax.shard_map(on_device, mesh=mesh, in_specs=in_specs, out_specs=out_specs, check_vma=False)
```
